128 devices in a mesh: leaf: 32 (over x, z, core), rhs: 4 (over y).
Axes of the slice: x: 4, y: 4, z: 4, core: 2. Of those that a mesh axis runs over, the one named last changes fastest.
Arguments:
- vectors: bfloat16 [128, 262144], P('rhs', 'leaf'), may hold values from -6 to 6
- near_blocks: bfloat16 [128, 2048, 2048], P(('leaf', 'rhs')), may hold values from -0.125 to 0.125
- leaf_basis: bfloat16 [128, 2048, 256], P(('leaf', 'rhs')), may hold values from -0.125 to 0.125
- lower_transfer: bfloat16 [128, 2, 256, 256], P(('leaf', 'rhs')), as said below
- lower_coupling: bfloat16 [128, 2, 256, 256], P(('leaf', 'rhs')), as said below
- upper_transfer: bfloat16 [62, 256, 256], replicated, may hold values from -0.3125 to 0.3125
- upper_coupling: bfloat16 [31, 256, 256], replicated, may hold values from -0.375 to 0.375
Outputs:
- product: float32 [128, 262144], P('rhs', 'leaf')
The draws below stay inside these ranges and needn't reach their ends.
Inputs may be any that keep to these rules, and one draw needn't show every extreme that they name: lower_transfer[d, l] is the same matrix for all d with equal d >> l. lower_coupling[d, l] is the same matrix for all d with equal d >> (l + 1).
All inputs are finite; a program needn't handle non-finite values.
Results may differ from the reference program's by a relative error of at most 0.002.
Values may be sent and summed in bfloat16 or wider, within the bound.
No kernel may reach another device: no remote copies, remote signals or barrier semaphores. Data moves between devices by JAX's collectives and lax.ppermute only.
A program may use at most 128 MiB of HBM per device.

```python
import math
import jax
import jax.numpy as jnp
from jax import lax

LEAF = 2048
RANK = 256
RHS = 128
NLEAF = 128
NS = 262144
LOW = 2
UPLEV = 5
UPNODES = 62
UPPAIRS = 31
N_LEAF = 32


def path_table(key, spread, offset):
    tables = []
    for height in range(LOW):
        count = NLEAF >> height + offset
        block = jax.random.uniform(jax.random.fold_in(key, height), (count, RANK, RANK), jnp.float32, -spread, spread)
        tables.append(jnp.repeat(block, 2 ** (height + offset), axis=0))
    return jnp.stack(tables, 1).astype(jnp.bfloat16)


def draw_lower_transfer(key, part):
    key = jax.random.fold_in(key, 11)
    return path_table(key, 1.47 / math.sqrt(RANK), 0)


def draw_lower_coupling(key, part):
    key = jax.random.fold_in(key, 23)
    return path_table(key, 1.73 / math.sqrt(RANK), 1)


def shard_levels(own_key, shape, cuts, least, high):
    def one(dim, blocks):
        heights = jax.random.uniform(jax.random.fold_in(jax.random.fold_in(own_key, 6), dim), (blocks,), jnp.float32, least / len(cuts), high / len(cuts))
        return jnp.repeat(jnp.exp(heights), shape[dim] // blocks).reshape((-1,) + (1,) * (len(shape) - dim - 1))

    loudness = one(*cuts[0])
    for cut in cuts[1:]:
        loudness = loudness * one(*cut)
    return loudness


def noise(stream_key, shape, deviation, most, pieces=(), held_as=jnp.bfloat16):
    factor_of = shard_levels(stream_key, shape, pieces, -0.22, 0.18) if pieces else 1.0
    values = jax.random.normal(stream_key, shape, jnp.float32) * deviation * factor_of
    return jnp.minimum(jnp.maximum(values, -most), most).astype(held_as)


def setup_inputs(seed: int = 0) -> dict:
    seeds = jax.random.split(jax.random.key(seed), 8)
    return {
        "vectors": noise(seeds[0], (RHS, NS), 1.0, 6.0, ((0, 4), (1, 32))),
        "near_blocks": noise(seeds[1], (NLEAF, LEAF, LEAF), LEAF ** -0.5, 0.125, ((0, 128),)),
        "leaf_basis": noise(seeds[2], (NLEAF, LEAF, RANK), LEAF ** -0.5, 0.125, ((0, 128),)),
        "lower_transfer": draw_lower_transfer(jax.random.fold_in(seeds[7], 71), 0),
        "lower_coupling": draw_lower_coupling(jax.random.fold_in(seeds[7], 71), 0),
        "upper_transfer": noise(seeds[5], (UPNODES, RANK, RANK), (7 * RANK // 5) ** -0.5, 0.3125),
        "upper_coupling": noise(seeds[6], (UPPAIRS, RANK, RANK), RANK ** -0.5, 0.375),
    }


def pairs_up(coeffs, transfer, coupling):
    proj = jnp.einsum("ncr,nrs->ncs", coeffs, transfer, precision=lax.Precision.HIGHEST)
    left_side = coeffs[0::2]
    right_side = coeffs[1::2]
    to_left = jnp.einsum("ncs,nrs->ncr", right_side, coupling, precision=lax.Precision.HIGHEST)
    to_right = jnp.einsum("ncr,nrs->ncs", left_side, coupling, precision=lax.Precision.HIGHEST)
    contrib = jnp.stack([to_left, to_right], 1).reshape(coeffs.shape)
    parent = proj[0::2] + proj[1::2]
    return parent, contrib


def reference(vectors, near_blocks, leaf_basis, lower_transfer, lower_coupling, upper_transfer, upper_coupling):
    columns = vectors.reshape(RHS, NLEAF, LEAF)
    indices = jnp.arange(NLEAF, dtype=jnp.int32)

    def leaf_coeffs(index):
        block = lax.dynamic_index_in_dim(columns, index, 1, False)
        return jnp.dot(block, leaf_basis[index], preferred_element_type=jnp.float32)

    coeffs = lax.map(leaf_coeffs, indices)
    tables = []
    for height in range(LOW):
        tables.append((lower_transfer[::2 ** height, height], lower_coupling[::2 ** (height + 1), height]))
    for height in range(UPLEV):
        count = N_LEAF >> height
        tables.append((upper_transfer[count - 2:2 * count - 2], upper_coupling[count // 2 - 1:count - 1]))
    saved = []
    for transfer, coupling in tables:
        transfer = transfer.astype(jnp.float32)
        parent, contrib = pairs_up(coeffs, transfer, coupling.astype(jnp.float32))
        saved.append((transfer, contrib))
        coeffs = parent
    downward = jnp.zeros((1, RHS, RANK), jnp.float32)
    for transfer, contrib in reversed(saved):
        spread = jnp.repeat(downward, 2, axis=0)
        downward = contrib + jnp.einsum("ncs,nrs->ncr", spread, transfer, precision=lax.Precision.HIGHEST)
    far_coeffs = downward.astype(jnp.bfloat16)

    def leaf_out(index):
        block = lax.dynamic_index_in_dim(columns, index, 1, False)
        near = lax.dot_general(block, near_blocks[index], (((1,), (1,)), ((), ())), preferred_element_type=jnp.float32)
        far = lax.dot_general(far_coeffs[index], leaf_basis[index], (((1,), (1,)), ((), ())), preferred_element_type=jnp.float32)
        return near + far

    outputs = lax.map(leaf_out, indices)
    return outputs.transpose(1, 0, 2).reshape(RHS, NS)
```

```python
import jax
import jax.numpy as jnp
from jax import lax
from jax.experimental import pallas as pl
from jax.experimental.pallas import tpu as pltpu
from jax.sharding import PartitionSpec as P

F32 = jnp.float32
BF16 = jnp.bfloat16
F16 = jnp.float16
VMEM = pl.BlockSpec(memory_space=pltpu.VMEM)
LIMIT = 32 * 2**20
EXTRA = 16


def swap(value, axis, mask):
    pairs = [(source, source ^ mask) for source in range(lax.axis_size(axis))]
    return lax.ppermute(value, axis, pairs)


def split(value):
    high = value.astype(BF16)
    return high, (value - high.astype(F32)).astype(BF16)


def dot(a, b):
    return jnp.dot(a, b, preferred_element_type=F32)


def dot_narrow(value, matrix):
    high, low = split(value)
    return dot(high, matrix) + dot(low, matrix)


def dot_wide(value, high_matrix, low_matrix):
    high, low = split(value)
    return dot(high, high_matrix) + (dot(low, high_matrix) + dot(high, low_matrix))


def encode(value):
    largest = jnp.max(jnp.abs(value), axis=0, keepdims=True)
    power = jnp.ceil(jnp.log2(jnp.maximum(largest, 1e-30))) - 14.0
    scaled = value * jnp.exp2(-power)
    return scaled, jnp.broadcast_to(power, (EXTRA, value.shape[1]))


def put_encoded(ref, value, start=0):
    rows = value.shape[0]
    scaled, power = encode(value)
    ref[start : start + rows, :] = scaled
    ref[start + rows : start + rows + EXTRA, :] = power


def decode(ref, rows, start=0):
    power = ref[start + rows : start + rows + 1, :]
    return ref[start : start + rows, :] * jnp.exp2(power)


def call(body, outs, operands, flops=0, moved=0, **more):
    return pl.pallas_call(
        body,
        out_shape=outs,
        compiler_params=pltpu.CompilerParams(vmem_limit_bytes=LIMIT),
        cost_estimate=pl.CostEstimate(flops=flops, bytes_accessed=moved, transcendentals=0),
        **more,
    )(*operands)


def shape(*dims, dtype=F32):
    return jax.ShapeDtypeStruct(dims, dtype)


def compose_body(rank, place, *refs):
    lower_t, lower_b = refs[0], refs[1]
    uppers = [ref[0] for ref in refs[2:14]]
    couplings = [ref[0] for ref in refs[14:19]]
    pair_ref, up_high, up_low, acc_high, acc_low, top_high, top_low = refs[19:26]
    rhs_pos, node = place[0], place[1]
    own2, sib2 = uppers[0:2]
    level3 = uppers[2:6]
    own4, sib4 = uppers[6:8]
    own5, _, third5, fourth5 = uppers[8:12]

    def oriented(coupling, is_right):
        wide = coupling.astype(F32)
        return jnp.where(is_right == 1, wide, wide.T).astype(BF16)

    def put(high_ref, low_ref, slot, value):
        high, low = split(value)
        high_ref[slot * rank : (slot + 1) * rank, :] = high
        low_ref[slot * rank : (slot + 1) * rank, :] = low
        return high, low

    def transposed(matrix):
        return matrix.astype(F32).T.astype(BF16)

    def times(matrix, parts):
        return dot(matrix, parts[0]) + dot(matrix, parts[1])

    pair_ref[:rank, :] = own2
    pair_ref[rank:, :] = sib2
    for slot, matrix in enumerate(level3):
        put(up_high, up_low, slot, dot(matrix, own4 if slot < 2 else sib4))

    put(acc_high, acc_low, 0, oriented(lower_b[0, 0], rhs_pos & 1).astype(F32))
    down = split(transposed(lower_t[0, 0]).astype(F32))
    put(acc_high, acc_low, 1, times(oriented(lower_b[0, 1], rhs_pos >> 1 & 1), down))
    down = split(times(transposed(lower_t[0, 1]), down))
    put(acc_high, acc_low, 2, times(oriented(couplings[0], node & 1), down))
    down = split(times(transposed(own2), down))
    put(acc_high, acc_low, 3, times(oriented(couplings[1], node >> 1 & 1), down))
    down = split(times(transposed(level3[0]), down))
    across = split(times(oriented(couplings[2], node >> 2 & 1), down))
    put(acc_high, acc_low, 4, times(level3[2], across))
    put(acc_high, acc_low, 5, times(level3[3], across))
    down = split(times(transposed(own4), down))
    put(top_high, top_low, 0, times(oriented(couplings[3], node >> 3 & 1), down))
    down = split(times(transposed(own5), down))
    across = split(times(oriented(couplings[4], node >> 4 & 1), down))
    put(top_high, top_low, 1, times(third5, across))
    put(top_high, top_low, 2, times(fourth5, across))


def compose(place, lower_transfer, lower_coupling, upper_transfer, upper_coupling):
    rank = lower_transfer.shape[-1]

    def upper(height, mask):
        return pl.BlockSpec(
            (1, rank, rank), lambda i, place: (((place[1] >> height) ^ mask) - 2, 0, 0)
        )

    def coupling(height):
        return pl.BlockSpec(
            (1, rank, rank), lambda i, place: ((place[1] >> (height + 1)) - 1, 0, 0)
        )

    def whole(array):
        return pl.BlockSpec(array.shape, lambda i, place: (0,) * array.ndim)

    picks = [(0, 0), (0, 1), (1, 0), (1, 1), (1, 2), (1, 3), (2, 0), (2, 1), (3, 0), (3, 1), (3, 2), (3, 3)]
    outs = [shape(n * rank, rank, dtype=BF16) for n in (2, 4, 4, 6, 6, 3, 3)]
    spec = pltpu.PrefetchScalarGridSpec(
        num_scalar_prefetch=1,
        grid=(1,),
        in_specs=[whole(lower_transfer), whole(lower_coupling)]
        + [upper(*pick) for pick in picks]
        + [coupling(height) for height in range(5)],
        out_specs=[pl.BlockSpec(out.shape, lambda i, place: (0, 0)) for out in outs],
    )

    def body(place_ref, *refs):
        compose_body(rank, place_ref, *refs)

    return call(
        body,
        outs,
        (place, lower_transfer, lower_coupling) + (upper_transfer,) * 12 + (upper_coupling,) * 5,
        flops=34 * 2 * rank**3,
        moved=40 * 2 * rank**2,
        grid_spec=spec,
    )


def shards(
    vectors, near_blocks, leaf_basis, lower_transfer, lower_coupling, upper_transfer, upper_coupling
):
    rhs_pos = lax.axis_index("rhs")
    leaf_pos = lax.axis_index("leaf")
    part = vectors.shape[0]
    leaf, rank = leaf_basis.shape[1:]
    total = part * lax.axis_size("rhs")
    place = jnp.stack([rhs_pos, leaf_pos + lax.axis_size("leaf")]).astype(jnp.int32)
    masks = (1, 3, 2)

    blocks = [lax.dynamic_slice(vectors, (0, (rhs_pos ^ mask) * leaf), (part, leaf)) for mask in (0,) + masks]
    came = [swap(block, "rhs", mask) for block, mask in zip(blocks[1:], masks)]

    pair, up_high, up_low, acc_high, acc_low, top_high, top_low = compose(
        place, lower_transfer, lower_coupling, upper_transfer, upper_coupling
    )

    def leaf_body(place_ref, own, first, second, third, basis, transfer, cols, sibling_msg, cousin_msg, kept):
        position = place_ref[0]
        for mask, ref in zip((0,) + masks, (own, first, second, third)):
            cols[pl.ds(pl.multiple_of((position ^ mask) * part, part), part), :] = ref[...]
        coeffs = dot(cols[...], basis[0])
        middle = dot_narrow(coeffs, transfer[0, 0])
        upward = dot_narrow(middle, transfer[0, 1])
        put_encoded(sibling_msg, coeffs)
        put_encoded(cousin_msg, middle)
        put_encoded(sibling_msg, upward, total + EXTRA)
        put_encoded(cousin_msg, upward, total + EXTRA)
        kept[...] = upward

    smem = pl.BlockSpec(memory_space=pltpu.SMEM)
    message = shape(2 * (total + EXTRA), rank)
    cols, sibling_msg, cousin_msg, upward = call(
        leaf_body,
        (shape(total, leaf, dtype=BF16), message, message, shape(total, rank)),
        (place, blocks[0], *came, leaf_basis, lower_transfer),
        flops=2 * total * leaf * rank,
        moved=2**21,
        in_specs=[smem] + [VMEM] * 6,
        out_specs=[VMEM] * 4,
    )
    sibling_msg = sibling_msg.astype(F16)
    cousin_msg = cousin_msg.astype(F16)
    from_sibling = swap(sibling_msg, "rhs", 1).astype(F32)
    from_third = swap(cousin_msg, "rhs", 3).astype(F32)
    from_second = swap(cousin_msg, "rhs", 2).astype(F32)

    steps = 8

    def near_body(cols_ref, block_ref, out_ref):
        out_ref[...] = lax.dot_general(
            cols_ref[...], block_ref[0], (((1,), (1,)), ((), ())), preferred_element_type=F32
        )

    near = call(
        near_body,
        shape(total, leaf),
        (cols, near_blocks),
        flops=2 * total * leaf * leaf,
        moved=2 * leaf * leaf + 6 * total * leaf,
        grid=(steps,),
        in_specs=[
            pl.BlockSpec((total, leaf), lambda i: (0, 0)),
            pl.BlockSpec((1, leaf // steps, leaf), lambda i: (0, i, 0)),
        ],
        out_specs=pl.BlockSpec((total, leaf // steps), lambda i: (0, i)),
    )

    def group_body(own, a, b, c, out):
        start = total + EXTRA
        out[...] = own[...] + decode(a, total, start) + (decode(b, total, start) + decode(c, total, start))

    group = call(
        group_body,
        shape(total, rank),
        (upward, from_sibling, from_third, from_second),
        moved=2**20,
        in_specs=[VMEM] * 4,
        out_specs=VMEM,
    )
    group_sib = swap(group, "leaf", 1)

    def chip_body(own, sibling, matrices, out, kept):
        value = dot_narrow(own[...], matrices[:rank, :]) + dot_narrow(sibling[...], matrices[rank:, :])
        kept[...] = value
        put_encoded(out, value)

    chip_msg, chip = call(
        chip_body,
        (shape(total + EXTRA, rank), shape(total, rank)),
        (group, group_sib, pair),
        flops=8 * total * rank * rank,
        moved=2**20,
        in_specs=[VMEM] * 3,
        out_specs=[VMEM] * 2,
    )
    chip_msg = chip_msg.astype(F16)
    chips = [swap(chip_msg, "leaf", 2 * mask).astype(F32) for mask in (1, 2, 3)]

    def line_body(own, a, b, c, high, low, out):
        value = jnp.concatenate([own[...]] + [decode(ref, total) for ref in (a, b, c)], axis=1)
        put_encoded(out, dot_wide(value, high[...], low[...]))

    line_msg = call(
        line_body,
        shape(total + EXTRA, rank),
        (chip, *chips, up_high, up_low),
        flops=24 * total * rank * rank,
        moved=2**21,
        in_specs=[VMEM] * 6,
        out_specs=VMEM,
    )
    line_msg = line_msg.astype(F16)
    lines = [swap(line_msg, "leaf", 8 * mask).astype(F32) for mask in (1, 2, 3)]

    def near_tree_body(y1, y3, y2, core, z1, z2, z3, high, low, out):
        value = jnp.concatenate(
            [decode(y1, total), decode(y3, total) + decode(y2, total), core[...]]
            + [decode(ref, total) for ref in (z1, z2, z3)],
            axis=1,
        )
        out[...] = dot_wide(value, high[...], low[...])

    partial = call(
        near_tree_body,
        shape(total, rank),
        (from_sibling, from_third, from_second, group_sib, *chips, acc_high, acc_low),
        flops=36 * total * rank * rank,
        moved=2**21,
        in_specs=[VMEM] * 9,
        out_specs=VMEM,
    )

    def last_body(place_ref, part_ref, a, b, c, high, low, basis, near_ref, own, first, second, third, both):
        value = jnp.concatenate([decode(ref, total) for ref in (a, b, c)], axis=1)
        coeffs = (part_ref[...] + dot_wide(value, high[...], low[...])).astype(BF16)
        far = lax.dot_general(coeffs, basis[0], (((1,), (1,)), ((), ())), preferred_element_type=F32)
        both[...] = near_ref[...] + far
        position = place_ref[0]
        for mask, ref in zip((0,) + masks, (own, first, second, third)):
            rows = both[pl.ds(pl.multiple_of((position ^ mask) * part, part), part), :]
            ref[...] = rows.astype(ref.dtype)

    sent = shape(part, leaf, dtype=BF16)
    own, *blocks = call(
        last_body,
        (shape(part, leaf), sent, sent, sent),
        (place, partial, *lines, top_high, top_low, leaf_basis, near),
        flops=2 * total * leaf * rank,
        moved=2**22,
        in_specs=[smem] + [VMEM] * 8,
        out_specs=[VMEM] * 4,
        scratch_shapes=[pltpu.VMEM((total, leaf), F32)],
    )
    blocks = [swap(block, "rhs", mask) for block, mask in zip(blocks, masks)]

    def join(place_ref, own_ref, first, second, third, out):
        position = place_ref[0]
        for mask, ref in zip((0,) + masks, (own_ref, first, second, third)):
            out[:, pl.ds(pl.multiple_of((position ^ mask) * leaf, leaf), leaf)] = ref[...].astype(F32)

    return call(
        join,
        shape(part, 4 * leaf),
        (place, own, *blocks),
        moved=2**21,
        in_specs=[smem] + [VMEM] * 4,
        out_specs=VMEM,
    )


def solution(mesh):
    in_specs = (
        P("rhs", "leaf"),
        P(("leaf", "rhs"), None, None),
        P(("leaf", "rhs"), None, None),
        P(("leaf", "rhs"), None, None, None),
        P(("leaf", "rhs"), None, None, None),
        P(),
        P(),
    )
    out_specs = P("rhs", "leaf")
    return jax.shard_map(shards, mesh=mesh, in_specs=in_specs, out_specs=out_specs, check_vma=False)
```

```python
import jax
import jax.numpy as jnp
from jax import lax
from jax.experimental import pallas as pl
from jax.experimental.pallas import tpu as pltpu
from jax.sharding import PartitionSpec as P

F32 = jnp.float32
BF16 = jnp.bfloat16
F16 = jnp.float16
VMEM = pl.BlockSpec(memory_space=pltpu.VMEM)
HBM = pl.BlockSpec(memory_space=pltpu.HBM)
LIMIT = 32 * 2**20
EXTRA = 16


def swap(value, axis, mask):
    pairs = [(source, source ^ mask) for source in range(lax.axis_size(axis))]
    return lax.ppermute(value, axis, pairs)


def split(value):
    high = value.astype(BF16)
    return high, (value - high.astype(F32)).astype(BF16)


def dot(a, b):
    return jnp.dot(a, b, preferred_element_type=F32)


def dot_narrow(value, matrix):
    high, low = split(value)
    return dot(high, matrix) + dot(low, matrix)


def dot_wide(value, high_matrix, low_matrix):
    high, low = split(value)
    return dot(high, high_matrix) + (dot(low, high_matrix) + dot(high, low_matrix))


def encode(value):
    largest = jnp.max(jnp.abs(value), axis=0, keepdims=True)
    power = jnp.ceil(jnp.log2(jnp.maximum(largest, 1e-30))) - 14.0
    scaled = value * jnp.exp2(-power)
    return scaled, jnp.broadcast_to(power, (EXTRA, value.shape[1]))


def put_encoded(ref, value):
    rows = value.shape[0]
    ref[:rows, :], ref[rows:, :] = encode(value)


def decode(ref):
    rows = ref.shape[0] - EXTRA
    return ref[:rows, :] * jnp.exp2(ref[rows : rows + 1, :])


def call(body, outs, operands, flops=0, moved=0, **more):
    return pl.pallas_call(
        body,
        out_shape=outs,
        compiler_params=pltpu.CompilerParams(vmem_limit_bytes=LIMIT),
        cost_estimate=pl.CostEstimate(flops=flops, bytes_accessed=moved, transcendentals=0),
        **more,
    )(*operands)


def shape(*dims, dtype=F32):
    return jax.ShapeDtypeStruct(dims, dtype)


def aligned(index, size):
    return pl.ds(pl.multiple_of(index * size, size), size)


def cut(vectors, leaf, masks):
    part = vectors.shape[0]

    def body(source, *rest):
        blocks, sems = rest[:-1], rest[-1]
        position = lax.axis_index("rhs")
        copies = [
            pltpu.make_async_copy(source.at[:, aligned(position ^ mask, leaf)], block, sems.at[slot])
            for slot, (mask, block) in enumerate(zip(masks, blocks))
        ]
        for copy in copies:
            copy.start()
        for copy in copies:
            copy.wait()

    count = len(masks)
    return call(
        body,
        [shape(part, leaf, dtype=BF16)] * count,
        (vectors,),
        moved=4 * count * part * leaf,
        in_specs=[HBM],
        out_specs=[VMEM] * count,
        scratch_shapes=[pltpu.SemaphoreType.DMA((count,))],
    )


def oriented(coupling, is_right):
    wide = coupling.astype(F32)
    return jnp.where(is_right == 1, wide, wide.T).astype(BF16)


def transposed(matrix):
    return matrix.astype(F32).T.astype(BF16)


def times(matrix, parts):
    return dot(matrix, parts[0]) + dot(matrix, parts[1])


PICKS = [(0, 0), (0, 1), (1, 0), (1, 1), (1, 2), (1, 3), (2, 0), (2, 1), (3, 0), (3, 2), (3, 3)]
COUPLED = 5


def compose(leaf_basis, lower_transfer, lower_coupling, upper_transfer, upper_coupling):
    leaf, rank = leaf_basis.shape[1:]
    n_up = len(PICKS)
    n_all = n_up + COUPLED

    def body(basis_hbm, low_t_hbm, low_b_hbm, up_t_hbm, up_b_hbm, *rest):
        basis, lower_t, pair, up_high, up_low, acc_high, acc_low, top_high, top_low = rest[:9]
        lower_b, uppers, couplings, sems = rest[9:]
        rhs_pos = lax.axis_index("rhs")
        node = lax.axis_index("leaf") + lax.axis_size("leaf")
        copies = []
        for slot, (height, mask) in enumerate(PICKS):
            copies.append((up_t_hbm.at[((node >> height) ^ mask) - 2], uppers.at[slot]))
        for height in range(COUPLED):
            copies.append((up_b_hbm.at[(node >> (height + 1)) - 1], couplings.at[height]))
        copies += [(low_t_hbm.at[0], lower_t), (low_b_hbm.at[0], lower_b), (basis_hbm.at[0], basis)]
        copies = [pltpu.make_async_copy(*pair_, sems.at[i]) for i, pair_ in enumerate(copies)]
        for copy in copies:
            copy.start()
        for copy in copies:
            copy.wait()

        def put(high_ref, low_ref, slot, value):
            high, low = split(value)
            high_ref[slot * rank : (slot + 1) * rank, :] = high
            low_ref[slot * rank : (slot + 1) * rank, :] = low

        own2, sib2 = uppers[0], uppers[1]
        level3 = [uppers[slot] for slot in range(2, 6)]
        own4, sib4, own5, third5, fourth5 = [uppers[slot] for slot in range(6, 11)]
        pair[:rank, :] = own2
        pair[rank:, :] = sib2
        for slot, matrix in enumerate(level3):
            put(up_high, up_low, slot, dot(matrix, own4 if slot < 2 else sib4))
        put(acc_high, acc_low, 0, oriented(lower_b[0], rhs_pos & 1).astype(F32))
        down = split(transposed(lower_t[0]).astype(F32))
        put(acc_high, acc_low, 1, times(oriented(lower_b[1], rhs_pos >> 1 & 1), down))
        down = split(times(transposed(lower_t[1]), down))
        put(acc_high, acc_low, 2, times(oriented(couplings[0], node & 1), down))
        down = split(times(transposed(own2), down))
        put(acc_high, acc_low, 3, times(oriented(couplings[1], node >> 1 & 1), down))
        down = split(times(transposed(level3[0]), down))
        across = split(times(oriented(couplings[2], node >> 2 & 1), down))
        put(acc_high, acc_low, 4, times(level3[2], across))
        put(acc_high, acc_low, 5, times(level3[3], across))
        down = split(times(transposed(own4), down))
        put(top_high, top_low, 0, times(oriented(couplings[3], node >> 3 & 1), down))
        down = split(times(transposed(own5), down))
        across = split(times(oriented(couplings[4], node >> 4 & 1), down))
        put(top_high, top_low, 1, times(third5, across))
        put(top_high, top_low, 2, times(fourth5, across))

    stacked = [shape(n * rank, rank, dtype=BF16) for n in (2, 4, 4, 6, 6, 3, 3)]
    return call(
        body,
        [shape(leaf, rank, dtype=BF16), shape(2, rank, rank, dtype=BF16)] + stacked,
        (leaf_basis, lower_transfer, lower_coupling, upper_transfer, upper_coupling),
        flops=34 * 2 * rank**3,
        moved=2**22,
        in_specs=[HBM] * 5,
        out_specs=[VMEM] * 9,
        scratch_shapes=[
            pltpu.VMEM((2, rank, rank), BF16),
            pltpu.VMEM((n_up, rank, rank), BF16),
            pltpu.VMEM((COUPLED, rank, rank), BF16),
            pltpu.SemaphoreType.DMA((n_all + 3,)),
        ],
    )


def shards(
    vectors, near_blocks, leaf_basis, lower_transfer, lower_coupling, upper_transfer, upper_coupling
):
    part = vectors.shape[0]
    leaf, rank = leaf_basis.shape[1:]
    total = part * lax.axis_size("rhs")
    masks = (0, 1, 3, 2)

    vectors = pltpu.with_memory_space_constraint(vectors, pltpu.HBM)
    blocks = cut(vectors, leaf, masks)
    came = [swap(block, "rhs", mask) for block, mask in zip(blocks[1:], masks[1:])]
    leaf_basis, lower_transfer, lower_coupling, upper_transfer, upper_coupling = [
        pltpu.with_memory_space_constraint(array, pltpu.HBM)
        for array in (leaf_basis, lower_transfer, lower_coupling, upper_transfer, upper_coupling)
    ]
    basis, low, pair, up_high, up_low, acc_high, acc_low, top_high, top_low = compose(
        leaf_basis, lower_transfer, lower_coupling, upper_transfer, upper_coupling
    )
    message = shape(total + EXTRA, rank)

    def leaf_body(own, first, second, third, basis_ref, transfer, cols, up_msg, own_msg, mid_msg, kept):
        position = lax.axis_index("rhs")
        for slot, ref in enumerate((own, first, second, third)):
            cols[slot * part : (slot + 1) * part, :] = ref[...]
        coeffs = dot(cols[...], basis_ref[...])
        middle = dot_narrow(coeffs, transfer[0])
        upward = dot_narrow(middle, transfer[1])
        for msg, value in ((up_msg, upward), (own_msg, coeffs), (mid_msg, middle)):
            scaled, power = encode(value)
            for slot, mask in enumerate(masks):
                msg[aligned(position ^ mask, part), :] = scaled[slot * part : (slot + 1) * part, :]
            msg[total:, :] = power
        for slot, mask in enumerate(masks):
            kept[aligned(position ^ mask, part), :] = upward[slot * part : (slot + 1) * part, :]

    cols, up_msg, own_msg, mid_msg, upward = call(
        leaf_body,
        (shape(total, leaf, dtype=BF16), message, message, message, shape(total, rank)),
        (blocks[0], *came, basis, low),
        flops=2 * total * leaf * rank,
        moved=2**21,
        in_specs=[VMEM] * 6,
        out_specs=[VMEM] * 5,
    )
    up_msg, own_msg, mid_msg = [msg.astype(F16) for msg in (up_msg, own_msg, mid_msg)]
    ups = [swap(up_msg, "rhs", mask).astype(F32) for mask in masks[1:]]
    def group_body(own, a, b, c, out):
        out[...] = own[...] + decode(a) + (decode(b) + decode(c))

    group = call(
        group_body,
        shape(total, rank),
        (upward, *ups),
        moved=2**20,
        in_specs=[VMEM] * 4,
        out_specs=VMEM,
    )
    group_sib = swap(group, "leaf", 1)

    def chip_body(own, sibling, matrices, out, kept):
        value = dot_narrow(own[...], matrices[:rank, :]) + dot_narrow(sibling[...], matrices[rank:, :])
        kept[...] = value
        put_encoded(out, value)

    chip_msg, chip = call(
        chip_body,
        (message, shape(total, rank)),
        (group, group_sib, pair),
        flops=8 * total * rank * rank,
        moved=2**20,
        in_specs=[VMEM] * 3,
        out_specs=[VMEM] * 2,
    )
    chip_msg = chip_msg.astype(F16)
    chips = [swap(chip_msg, "leaf", 2 * mask) for mask in (1, 3, 2)]
    own_msg, mid_msg, chips[0] = lax.optimization_barrier((own_msg, mid_msg, chips[0]))
    chips = [chips[slot].astype(F32) for slot in (0, 2, 1)]
    mids = [swap(own_msg, "rhs", 1).astype(F32)] + [swap(mid_msg, "rhs", mask).astype(F32) for mask in (3, 2)]


    def line_body(own, a, b, c, high, low, out):
        value = jnp.concatenate([own[...]] + [decode(ref) for ref in (a, b, c)], axis=1)
        put_encoded(out, dot_wide(value, high[...], low[...]))

    line_msg = call(
        line_body,
        message,
        (chip, *chips, up_high, up_low),
        flops=24 * total * rank * rank,
        moved=2**21,
        in_specs=[VMEM] * 6,
        out_specs=VMEM,
    )
    line_msg, cols = lax.optimization_barrier((line_msg.astype(F16), cols))
    lines = [swap(line_msg, "leaf", 8 * mask).astype(F32) for mask in (1, 2, 3)]

    steps = 8

    def near_body(cols_ref, block_ref, y1, y3, y2, core, z1, z2, z3, high, low, out_ref, part_out):
        out_ref[...] = lax.dot_general(
            cols_ref[...], block_ref[0], (((1,), (1,)), ((), ())), preferred_element_type=F32
        )

        @pl.when(pl.program_id(0) == 0)
        def _():
            value = jnp.concatenate(
                [decode(y1), decode(y3) + decode(y2), core[...]] + [decode(ref) for ref in (z1, z2, z3)],
                axis=1,
            )
            part_out[...] = dot_wide(value, high[...], low[...])

    near, partial = call(
        near_body,
        (shape(total, leaf), shape(total, rank)),
        (cols, near_blocks, *mids, group_sib, *chips, acc_high, acc_low),
        flops=2 * total * leaf * leaf,
        moved=2 * leaf * leaf + 6 * total * leaf,
        grid=(steps,),
        in_specs=[VMEM, pl.BlockSpec((1, leaf // steps, leaf), lambda i: (0, i, 0))] + [VMEM] * 9,
        out_specs=[pl.BlockSpec((total, leaf // steps), lambda i: (0, i)), VMEM],
    )

    def last_body(part_ref, a, b, c, high, low, basis_ref, near_ref, own, first, second, third, inner):
        position = lax.axis_index("rhs")
        value = jnp.concatenate([decode(ref) for ref in (a, b, c)], axis=1)
        inner[...] = part_ref[...] + dot_wide(value, high[...], low[...])
        coeffs = jnp.concatenate([inner[aligned(position ^ mask, part), :] for mask in masks], axis=0)
        far = lax.dot_general(
            coeffs.astype(BF16), basis_ref[...], (((1,), (1,)), ((), ())), preferred_element_type=F32
        )
        for slot, ref in enumerate((own, first, second, third)):
            rows = slice(slot * part, (slot + 1) * part)
            ref[...] = (near_ref[rows, :] + far[rows, :]).astype(ref.dtype)

    sent = shape(part, leaf, dtype=BF16)
    own, *blocks = call(
        last_body,
        (shape(part, leaf), sent, sent, sent),
        (partial, *lines, top_high, top_low, basis, near),
        flops=2 * total * leaf * rank,
        moved=2**22,
        in_specs=[VMEM] * 8,
        out_specs=[VMEM] * 4,
        scratch_shapes=[pltpu.VMEM((total, rank), F32)],
    )
    blocks = [swap(block, "rhs", mask) for block, mask in zip(blocks, masks[1:])]

    def join_body(count, slots, *refs):
        blocks, out, wide, sems = refs[:count], refs[-3], refs[-2], refs[-1]
        position = lax.axis_index("rhs")
        copies = []
        for i, (block, slot) in enumerate(zip(blocks, slots)):
            wide[i] = block[...].astype(F32)
            target = out.at[:, aligned(position ^ masks[slot], leaf)]
            copies.append(pltpu.make_async_copy(wide.at[i], target, sems.at[i]))
            copies[-1].start()
        for copy in copies:
            copy.wait()

    def join(blocks, slots, under=None):
        count = len(blocks)

        def body(*refs):
            join_body(count, slots, *refs)

        return call(
            body,
            shape(part, 4 * leaf),
            (*blocks,) if under is None else (*blocks, under),
            moved=6 * part * leaf * count,
            in_specs=[VMEM] * count + ([] if under is None else [HBM]),
            out_specs=HBM,
            scratch_shapes=[pltpu.VMEM((count, part, leaf), F32), pltpu.SemaphoreType.DMA((count,))],
            input_output_aliases={} if under is None else {count: 0},
        )

    most = join((own, blocks[0], blocks[1]), (0, 1, 2))
    return join((blocks[2],), (3,), most)


def solution(mesh):
    in_specs = (
        P("rhs", "leaf"),
        P(("leaf", "rhs"), None, None),
        P(("leaf", "rhs"), None, None),
        P(("leaf", "rhs"), None, None, None),
        P(("leaf", "rhs"), None, None, None),
        P(),
        P(),
    )
    out_specs = P("rhs", "leaf")
    return jax.shard_map(shards, mesh=mesh, in_specs=in_specs, out_specs=out_specs, check_vma=False)
```

```python
import jax
import jax.numpy as jnp
from jax import lax
from jax.experimental import pallas as pl
from jax.experimental.pallas import tpu as pltpu
from jax.sharding import PartitionSpec as P

F32 = jnp.float32
BF16 = jnp.bfloat16
F16 = jnp.float16
VMEM = pl.BlockSpec(memory_space=pltpu.VMEM)
HBM = pl.BlockSpec(memory_space=pltpu.HBM)
LIMIT = 32 * 2**20
EXTRA = 16


def swap(value, axis, mask):
    pairs = [(source, source ^ mask) for source in range(lax.axis_size(axis))]
    return lax.ppermute(value, axis, pairs)


def split(value):
    high = value.astype(BF16)
    return high, (value - high.astype(F32)).astype(BF16)


def dot(a, b):
    return jnp.dot(a, b, preferred_element_type=F32)


def dot_narrow(value, matrix):
    high, low = split(value)
    return dot(high, matrix) + dot(low, matrix)


def dot_wide(value, high_matrix, low_matrix):
    high, low = split(value)
    return dot(high, high_matrix) + (dot(low, high_matrix) + dot(high, low_matrix))


def encode(value):
    largest = jnp.max(jnp.abs(value), axis=0, keepdims=True)
    power = jnp.ceil(jnp.log2(jnp.maximum(largest, 1e-30))) - 14.0
    scaled = value * jnp.exp2(-power)
    return scaled, jnp.broadcast_to(power, (EXTRA, value.shape[1]))


def put_encoded(ref, value):
    rows = value.shape[0]
    ref[:rows, :], ref[rows:, :] = encode(value)


def decode(ref):
    rows = ref.shape[0] - EXTRA
    return ref[:rows, :] * jnp.exp2(ref[rows : rows + 1, :])


def call(body, outs, operands, flops=0, moved=0, **more):
    return pl.pallas_call(
        body,
        out_shape=outs,
        compiler_params=pltpu.CompilerParams(vmem_limit_bytes=LIMIT),
        cost_estimate=pl.CostEstimate(flops=flops, bytes_accessed=moved, transcendentals=0),
        **more,
    )(*operands)


def shape(*dims, dtype=F32):
    return jax.ShapeDtypeStruct(dims, dtype)


def aligned(index, size):
    return pl.ds(pl.multiple_of(index * size, size), size)


def cut(vectors, leaf, masks):
    part = vectors.shape[0]

    def body(source, *rest):
        blocks, sems = rest[:-1], rest[-1]
        position = lax.axis_index("rhs")
        copies = [
            pltpu.make_async_copy(source.at[:, aligned(position ^ mask, leaf)], block, sems.at[slot])
            for slot, (mask, block) in enumerate(zip(masks, blocks))
        ]
        for copy in copies:
            copy.start()
        for copy in copies:
            copy.wait()

    count = len(masks)
    return call(
        body,
        [shape(part, leaf, dtype=BF16)] * count,
        (vectors,),
        moved=4 * count * part * leaf,
        in_specs=[HBM],
        out_specs=[VMEM] * count,
        scratch_shapes=[pltpu.SemaphoreType.DMA((count,))],
    )


def oriented(coupling, is_right):
    wide = coupling.astype(F32)
    return jnp.where(is_right == 1, wide, wide.T).astype(BF16)


def transposed(matrix):
    return matrix.astype(F32).T.astype(BF16)


def times(matrix, parts):
    return dot(matrix, parts[0]) + dot(matrix, parts[1])


PICKS = [(0, 0), (0, 1), (1, 0), (1, 1), (1, 2), (1, 3), (2, 0), (2, 1), (3, 0), (3, 2), (3, 3)]
COUPLED = 5


def compose(leaf_basis, lower_transfer, lower_coupling, upper_transfer, upper_coupling):
    leaf, rank = leaf_basis.shape[1:]
    n_up = len(PICKS)
    n_all = n_up + COUPLED

    def body(basis_hbm, low_t_hbm, low_b_hbm, up_t_hbm, up_b_hbm, *rest):
        basis, lower_t, pair, up_high, up_low, acc_high, acc_low, top_high, top_low = rest[:9]
        lower_b, uppers, couplings, sems = rest[9:]
        rhs_pos = lax.axis_index("rhs")
        node = lax.axis_index("leaf") + lax.axis_size("leaf")
        copies = []
        for slot, (height, mask) in enumerate(PICKS):
            copies.append((up_t_hbm.at[((node >> height) ^ mask) - 2], uppers.at[slot]))
        for height in range(COUPLED):
            copies.append((up_b_hbm.at[(node >> (height + 1)) - 1], couplings.at[height]))
        copies += [(low_t_hbm.at[0], lower_t), (low_b_hbm.at[0], lower_b), (basis_hbm.at[0], basis)]
        copies = [pltpu.make_async_copy(*pair_, sems.at[i]) for i, pair_ in enumerate(copies)]
        for copy in copies:
            copy.start()
        for copy in copies:
            copy.wait()

        def put(high_ref, low_ref, slot, value):
            high, low = split(value)
            high_ref[slot * rank : (slot + 1) * rank, :] = high
            low_ref[slot * rank : (slot + 1) * rank, :] = low

        own2, sib2 = uppers[0], uppers[1]
        level3 = [uppers[slot] for slot in range(2, 6)]
        own4, sib4, own5, third5, fourth5 = [uppers[slot] for slot in range(6, 11)]
        pair[:rank, :] = own2
        pair[rank:, :] = sib2
        for slot, matrix in enumerate(level3):
            put(up_high, up_low, slot, dot(matrix, own4 if slot < 2 else sib4))
        put(acc_high, acc_low, 0, oriented(lower_b[0], rhs_pos & 1).astype(F32))
        down = split(transposed(lower_t[0]).astype(F32))
        put(acc_high, acc_low, 1, times(oriented(lower_b[1], rhs_pos >> 1 & 1), down))
        down = split(times(transposed(lower_t[1]), down))
        put(acc_high, acc_low, 2, times(oriented(couplings[0], node & 1), down))
        down = split(times(transposed(own2), down))
        put(acc_high, acc_low, 3, times(oriented(couplings[1], node >> 1 & 1), down))
        down = split(times(transposed(level3[0]), down))
        across = split(times(oriented(couplings[2], node >> 2 & 1), down))
        put(acc_high, acc_low, 4, times(level3[2], across))
        put(acc_high, acc_low, 5, times(level3[3], across))
        down = split(times(transposed(own4), down))
        put(top_high, top_low, 0, times(oriented(couplings[3], node >> 3 & 1), down))
        down = split(times(transposed(own5), down))
        across = split(times(oriented(couplings[4], node >> 4 & 1), down))
        put(top_high, top_low, 1, times(third5, across))
        put(top_high, top_low, 2, times(fourth5, across))

    stacked = [shape(n * rank, rank, dtype=BF16) for n in (2, 4, 4, 6, 6, 3, 3)]
    return call(
        body,
        [shape(leaf, rank, dtype=BF16), shape(2, rank, rank, dtype=BF16)] + stacked,
        (leaf_basis, lower_transfer, lower_coupling, upper_transfer, upper_coupling),
        flops=34 * 2 * rank**3,
        moved=2**22,
        in_specs=[HBM] * 5,
        out_specs=[VMEM] * 9,
        scratch_shapes=[
            pltpu.VMEM((2, rank, rank), BF16),
            pltpu.VMEM((n_up, rank, rank), BF16),
            pltpu.VMEM((COUPLED, rank, rank), BF16),
            pltpu.SemaphoreType.DMA((n_all + 3,)),
        ],
    )


def shards(
    vectors, near_blocks, leaf_basis, lower_transfer, lower_coupling, upper_transfer, upper_coupling
):
    part = vectors.shape[0]
    leaf, rank = leaf_basis.shape[1:]
    total = part * lax.axis_size("rhs")
    masks = (0, 1, 3, 2)

    vectors = pltpu.with_memory_space_constraint(vectors, pltpu.HBM)
    blocks = cut(vectors, leaf, masks)
    came = [swap(block, "rhs", mask) for block, mask in zip(blocks[1:], masks[1:])]
    leaf_basis, lower_transfer, lower_coupling, upper_transfer, upper_coupling = [
        pltpu.with_memory_space_constraint(array, pltpu.HBM)
        for array in (leaf_basis, lower_transfer, lower_coupling, upper_transfer, upper_coupling)
    ]
    basis, low, pair, up_high, up_low, acc_high, acc_low, top_high, top_low = compose(
        leaf_basis, lower_transfer, lower_coupling, upper_transfer, upper_coupling
    )
    message = shape(total + EXTRA, rank)

    def leaf_body(own, first, second, third, basis_ref, transfer, cols, up_msg, low_msg, up_ref, mid_ref):
        position = lax.axis_index("rhs")
        for slot, ref in enumerate((own, first, second, third)):
            cols[slot * part : (slot + 1) * part, :] = ref[...]
        coeffs = dot(cols[...], basis_ref[...])
        middle = dot_narrow(coeffs, transfer[0])
        upward = dot_narrow(middle, transfer[1])

        def place(ref, value, start=0):
            for slot, mask in enumerate(masks):
                rows = value[slot * part : (slot + 1) * part, :]
                ref[pl.ds(pl.multiple_of(start + (position ^ mask) * part, 16), part), :] = rows

        for msg, value, start in ((up_msg, upward, 0), (low_msg, coeffs, 0), (low_msg, middle, total + EXTRA)):
            scaled, power = encode(value)
            place(msg, scaled, start)
            msg[start + total : start + total + EXTRA, :] = power
        place(up_ref, upward)
        place(mid_ref, middle)

    plain = shape(total, rank)
    cols, up_msg, low_msg, upward, middle = call(
        leaf_body,
        (shape(total, leaf, dtype=BF16), message, shape(2 * (total + EXTRA), rank), plain, plain),
        (blocks[0], *came, basis, low),
        flops=2 * total * leaf * rank,
        moved=2**21,
        in_specs=[VMEM] * 6,
        out_specs=[VMEM] * 5,
    )
    up_msg, low_msg = up_msg.astype(F16), low_msg.astype(F16)
    ups = [swap(up_msg, "rhs", mask).astype(F32) for mask in masks[1:]]
    low_sib = swap(low_msg, "rhs", 1).astype(F32)

    def near_half(cols, half):
        width = leaf // 8

        def body(cols_ref, block_ref, out_ref):
            for step in range(4):
                rows = block_ref[0, (4 * half + step) * width : (4 * half + step + 1) * width, :]
                out_ref[:, step * width : (step + 1) * width] = lax.dot_general(
                    cols_ref[...], rows, (((1,), (1,)), ((), ())), preferred_element_type=F32
                )

        return call(
            body,
            shape(total, leaf // 2),
            (cols, near_blocks),
            flops=total * leaf * leaf,
            moved=leaf * leaf + 3 * total * leaf,
            in_specs=[VMEM] * 2,
            out_specs=VMEM,
        )

    near_left = near_half(cols, 0)
    ups, near_left = lax.optimization_barrier((ups, near_left))

    def group_body(own, a, b, c, out):
        out[...] = own[...] + decode(a) + (decode(b) + decode(c))

    group = call(
        group_body,
        plain,
        (upward, *ups),
        moved=2**20,
        in_specs=[VMEM] * 4,
        out_specs=VMEM,
    )
    group_sib = swap(group, "leaf", 1)

    def chip_body(own, sibling, matrices, mid_ref, low_ref, out, kept, cousin_msg):
        value = dot_narrow(own[...], matrices[:rank, :]) + dot_narrow(sibling[...], matrices[rank:, :])
        kept[...] = value
        put_encoded(out, value)
        put_encoded(cousin_msg, mid_ref[...] + decode(low_ref.at[total + EXTRA :, :]))

    chip_msg, chip, cousin_msg = call(
        chip_body,
        (message, plain, message),
        (group, group_sib, pair, middle, low_sib),
        flops=8 * total * rank * rank,
        moved=2**20,
        in_specs=[VMEM] * 5,
        out_specs=[VMEM] * 3,
    )
    chip_msg, cols = lax.optimization_barrier((chip_msg.astype(F16), cols))
    chips = [swap(chip_msg, "leaf", 2 * mask).astype(F32) for mask in (1, 2, 3)]
    cousin = swap(cousin_msg.astype(F16), "rhs", 3).astype(F32)
    near_right = near_half(cols, 1)
    chips, cousin, near_right = lax.optimization_barrier((chips, cousin, near_right))

    def line_body(own, a, b, c, high, low, out):
        value = jnp.concatenate([own[...]] + [decode(ref) for ref in (a, b, c)], axis=1)
        put_encoded(out, dot_wide(value, high[...], low[...]))

    line_msg = call(
        line_body,
        message,
        (chip, *chips, up_high, up_low),
        flops=24 * total * rank * rank,
        moved=2**21,
        in_specs=[VMEM] * 6,
        out_specs=VMEM,
    )
    line_msg = line_msg.astype(F16)
    lines = [swap(line_msg, "leaf", 8 * mask).astype(F32) for mask in (1, 2, 3)]

    def partial_body(sibling, others, core, z1, z2, z3, high, low, out):
        value = jnp.concatenate(
            [decode(sibling.at[: total + EXTRA, :]), decode(others), core[...]]
            + [decode(ref) for ref in (z1, z2, z3)],
            axis=1,
        )
        out[...] = dot_wide(value, high[...], low[...])

    partial = call(
        partial_body,
        plain,
        (low_sib, cousin, group_sib, *chips, acc_high, acc_low),
        flops=36 * total * rank * rank,
        moved=2**21,
        in_specs=[VMEM] * 8,
        out_specs=VMEM,
    )

    def last_body(part_ref, a, b, c, high, low, basis_ref, left, right, own, first, second, third, inner):
        position = lax.axis_index("rhs")
        value = jnp.concatenate([decode(ref) for ref in (a, b, c)], axis=1)
        inner[...] = part_ref[...] + dot_wide(value, high[...], low[...])
        coeffs = jnp.concatenate([inner[aligned(position ^ mask, part), :] for mask in masks], axis=0)
        far = lax.dot_general(
            coeffs.astype(BF16), basis_ref[...], (((1,), (1,)), ((), ())), preferred_element_type=F32
        )
        for slot, ref in enumerate((own, first, second, third)):
            rows = slice(slot * part, (slot + 1) * part)
            ref[:, : leaf // 2] = (left[rows, :] + far[rows, : leaf // 2]).astype(ref.dtype)
            ref[:, leaf // 2 :] = (right[rows, :] + far[rows, leaf // 2 :]).astype(ref.dtype)

    sent = shape(part, leaf, dtype=BF16)
    own, *blocks = call(
        last_body,
        (shape(part, leaf), sent, sent, sent),
        (partial, *lines, top_high, top_low, basis, near_left, near_right),
        flops=2 * total * leaf * rank,
        moved=2**22,
        in_specs=[VMEM] * 9,
        out_specs=[VMEM] * 4,
        scratch_shapes=[pltpu.VMEM((total, rank), F32)],
    )
    blocks = [swap(block, "rhs", mask) for block, mask in zip(blocks, masks[1:])]

    def join_body(count, slots, *refs):
        blocks, out, wide, sems = refs[:count], refs[-3], refs[-2], refs[-1]
        position = lax.axis_index("rhs")
        copies = []
        for i, (block, slot) in enumerate(zip(blocks, slots)):
            wide[i] = block[...].astype(F32)
            target = out.at[:, aligned(position ^ masks[slot], leaf)]
            copies.append(pltpu.make_async_copy(wide.at[i], target, sems.at[i]))
            copies[-1].start()
        for copy in copies:
            copy.wait()

    def join(blocks, slots, under=None):
        count = len(blocks)

        def body(*refs):
            join_body(count, slots, *refs)

        return call(
            body,
            shape(part, 4 * leaf),
            (*blocks,) if under is None else (*blocks, under),
            moved=6 * part * leaf * count,
            in_specs=[VMEM] * count + ([] if under is None else [HBM]),
            out_specs=HBM,
            scratch_shapes=[pltpu.VMEM((count, part, leaf), F32), pltpu.SemaphoreType.DMA((count,))],
            input_output_aliases={} if under is None else {count: 0},
        )

    most = join((own, blocks[0], blocks[1]), (0, 1, 2))
    return join((blocks[2],), (3,), most)


def solution(mesh):
    in_specs = (
        P("rhs", "leaf"),
        P(("leaf", "rhs"), None, None),
        P(("leaf", "rhs"), None, None),
        P(("leaf", "rhs"), None, None, None),
        P(("leaf", "rhs"), None, None, None),
        P(),
        P(),
    )
    out_specs = P("rhs", "leaf")
    return jax.shard_map(shards, mesh=mesh, in_specs=in_specs, out_specs=out_specs, check_vma=False)
```

```python
import jax
import jax.numpy as jnp
from jax import lax
from jax.experimental import pallas as pl
from jax.experimental.pallas import tpu as pltpu
from jax.sharding import PartitionSpec as P

F32 = jnp.float32
BF16 = jnp.bfloat16
F16 = jnp.float16
VMEM = pl.BlockSpec(memory_space=pltpu.VMEM)
HBM = pl.BlockSpec(memory_space=pltpu.HBM)
LIMIT = 32 * 2**20
EXTRA = 16


def swap(value, axis, mask):
    pairs = [(source, source ^ mask) for source in range(lax.axis_size(axis))]
    return lax.ppermute(value, axis, pairs)


def split(value):
    high = value.astype(BF16)
    return high, (value - high.astype(F32)).astype(BF16)


def dot(a, b):
    return jnp.dot(a, b, preferred_element_type=F32)


def dot_narrow(value, matrix):
    high, low = split(value)
    return dot(high, matrix) + dot(low, matrix)


def dot_wide(value, high_matrix, low_matrix):
    high, low = split(value)
    return dot(high, high_matrix) + (dot(low, high_matrix) + dot(high, low_matrix))


def encode(value):
    largest = jnp.max(jnp.abs(value), axis=0, keepdims=True)
    power = jnp.ceil(jnp.log2(jnp.maximum(largest, 1e-30))) - 14.0
    scaled = value * jnp.exp2(-power)
    return scaled, jnp.broadcast_to(power, (EXTRA, value.shape[1]))


def put_encoded(ref, value):
    rows = value.shape[0]
    ref[:rows, :], ref[rows:, :] = encode(value)


def decode(ref):
    rows = ref.shape[0] - EXTRA
    return ref[:rows, :] * jnp.exp2(ref[rows : rows + 1, :])


def call(body, outs, operands, flops=0, moved=0, **more):
    return pl.pallas_call(
        body,
        out_shape=outs,
        compiler_params=pltpu.CompilerParams(vmem_limit_bytes=LIMIT),
        cost_estimate=pl.CostEstimate(flops=flops, bytes_accessed=moved, transcendentals=0),
        **more,
    )(*operands)


def shape(*dims, dtype=F32):
    return jax.ShapeDtypeStruct(dims, dtype)


def line(message, axis, step, beside=None):
    leaves, group = lax.axis_size("leaf"), lax.axis_size("rhs")
    if axis == "leaf":
        pairs = [(i, i ^ step * (1 + (i & 1))) for i in range(leaves)]
    else:
        axis = ("leaf", "rhs")
        pairs = [(i * group + j, i * group + (j ^ (1 + (i & 1)))) for i in range(leaves) for j in range(group)]
    mine = lax.ppermute(message, axis, pairs)
    third = swap(message, "leaf" if axis == "leaf" else "rhs", 3 * step)
    if beside is not None:
        mine, beside = lax.optimization_barrier((mine, beside))
    return [mine, swap(mine, "leaf", 1), third], beside


def aligned(index, size):
    return pl.ds(pl.multiple_of(index * size, size), size)


def cut(vectors, leaf, masks):
    part = vectors.shape[0]

    def body(source, *rest):
        blocks, sems = rest[:-1], rest[-1]
        position = lax.axis_index("rhs")
        copies = [
            pltpu.make_async_copy(source.at[:, aligned(position ^ mask, leaf)], block, sems.at[slot])
            for slot, (mask, block) in enumerate(zip(masks, blocks))
        ]
        for copy in copies:
            copy.start()
        for copy in copies:
            copy.wait()

    count = len(masks)
    return call(
        body,
        [shape(part, leaf, dtype=BF16)] * count,
        (vectors,),
        moved=4 * count * part * leaf,
        in_specs=[HBM],
        out_specs=[VMEM] * count,
        scratch_shapes=[pltpu.SemaphoreType.DMA((count,))],
    )


def oriented(coupling, is_right):
    wide = coupling.astype(F32)
    return jnp.where(is_right == 1, wide, wide.T).astype(BF16)


def transposed(matrix):
    return matrix.astype(F32).T.astype(BF16)


def times(matrix, parts):
    return dot(matrix, parts[0]) + dot(matrix, parts[1])


PICKS = [(0, 0), (0, 1), (1, 0), (1, 1), (1, 2), (1, 3), (2, 0), (2, 1), (3, 0), (3, 2), (3, 3)]
COUPLED = 5


def compose(leaf_basis, lower_transfer, lower_coupling, upper_transfer, upper_coupling):
    leaf, rank = leaf_basis.shape[1:]
    n_up = len(PICKS)
    n_all = n_up + COUPLED

    def body(basis_hbm, low_t_hbm, low_b_hbm, up_t_hbm, up_b_hbm, *rest):
        basis, lower_t, pair, up_high, up_low, acc_high, acc_low, top_high, top_low = rest[:9]
        lower_b, uppers, couplings, sems = rest[9:]
        rhs_pos = lax.axis_index("rhs")
        node = lax.axis_index("leaf") + lax.axis_size("leaf")
        copies = {}

        def start(name, source, target):
            copies[name] = pltpu.make_async_copy(source, target, sems.at[len(copies)])
            copies[name].start()

        start("t", low_t_hbm.at[0], lower_t)
        start("b", low_b_hbm.at[0], lower_b)
        for slot, (height, mask) in enumerate(PICKS):
            start(slot, up_t_hbm.at[((node >> height) ^ mask) - 2], uppers.at[slot])
        for height in range(COUPLED):
            start(n_up + height, up_b_hbm.at[(node >> (height + 1)) - 1], couplings.at[height])
        start("basis", basis_hbm.at[0], basis)

        def upper(slot):
            copies[slot].wait()
            return uppers[slot]

        def coupling(height):
            copies[n_up + height].wait()
            return couplings[height]

        def put(high_ref, low_ref, slot, value):
            high, low = split(value)
            high_ref[aligned(slot, rank), :] = high
            low_ref[aligned(slot, rank), :] = low

        first = node & 1
        second = 1 - first

        copies["t"].wait()
        copies["b"].wait()
        put(acc_high, acc_low, 0, oriented(lower_b[0], rhs_pos & 1).astype(F32))
        down = split(transposed(lower_t[0]).astype(F32))
        put(acc_high, acc_low, 1, times(oriented(lower_b[1], rhs_pos >> 1 & 1), down))
        down = split(times(transposed(lower_t[1]), down))
        own2 = upper(0)
        pair[:rank, :] = own2
        pair[rank:, :] = upper(1)
        level3 = [upper(slot) for slot in range(2, 6)]
        own4, sib4, own5, third5, fourth5 = [upper(slot) for slot in range(6, 11)]
        put(acc_high, acc_low, 2, times(oriented(coupling(0), node & 1), down))
        down = split(times(transposed(own2), down))
        put(acc_high, acc_low, 3 + first, times(oriented(coupling(1), node >> 1 & 1), down))
        down = split(times(transposed(level3[0]), down))
        across = split(times(oriented(coupling(2), node >> 2 & 1), down))
        put(acc_high, acc_low, 3 + second, times(level3[2], across))
        put(acc_high, acc_low, 5, times(level3[3], across))
        down = split(times(transposed(own4), down))
        put(top_high, top_low, first, times(oriented(coupling(3), node >> 3 & 1), down))
        down = split(times(transposed(own5), down))
        across = split(times(oriented(coupling(4), node >> 4 & 1), down))
        put(top_high, top_low, second, times(third5, across))
        put(top_high, top_low, 2, times(fourth5, across))
        put(up_high, up_low, 0, dot(level3[0], own4))
        put(up_high, up_low, 1 + first, dot(level3[1], own4))
        put(up_high, up_low, 1 + second, dot(level3[2], sib4))
        put(up_high, up_low, 3, dot(level3[3], sib4))
        copies["basis"].wait()

    stacked = [shape(n * rank, rank, dtype=BF16) for n in (2, 4, 4, 6, 6, 3, 3)]
    return call(
        body,
        [shape(leaf, rank, dtype=BF16), shape(2, rank, rank, dtype=BF16)] + stacked,
        (leaf_basis, lower_transfer, lower_coupling, upper_transfer, upper_coupling),
        flops=34 * 2 * rank**3,
        moved=2**22,
        in_specs=[HBM] * 5,
        out_specs=[VMEM] * 9,
        scratch_shapes=[
            pltpu.VMEM((2, rank, rank), BF16),
            pltpu.VMEM((n_up, rank, rank), BF16),
            pltpu.VMEM((COUPLED, rank, rank), BF16),
            pltpu.SemaphoreType.DMA((n_all + 3,)),
        ],
    )


def shards(
    vectors, near_blocks, leaf_basis, lower_transfer, lower_coupling, upper_transfer, upper_coupling
):
    part = vectors.shape[0]
    leaf, rank = leaf_basis.shape[1:]
    total = part * lax.axis_size("rhs")
    masks = (0, 1, 3, 2)

    vectors = pltpu.with_memory_space_constraint(vectors, pltpu.HBM)
    blocks = cut(vectors, leaf, masks)
    came = [swap(block, "rhs", mask) for block, mask in zip(blocks[1:], masks[1:])]
    leaf_basis, lower_transfer, lower_coupling, upper_transfer, upper_coupling = [
        pltpu.with_memory_space_constraint(array, pltpu.HBM)
        for array in (leaf_basis, lower_transfer, lower_coupling, upper_transfer, upper_coupling)
    ]
    basis, low, pair, up_high, up_low, acc_high, acc_low, top_high, top_low = compose(
        leaf_basis, lower_transfer, lower_coupling, upper_transfer, upper_coupling
    )
    message = shape(total + EXTRA, rank)

    def leaf_body(own, first, second, third, basis_ref, transfer, cols, up_msg, low_msg, up_ref, mid_ref):
        position = lax.axis_index("rhs")
        for slot, ref in enumerate((own, first, second, third)):
            cols[slot * part : (slot + 1) * part, :] = ref[...]
        coeffs = dot(cols[...], basis_ref[...])
        middle = dot_narrow(coeffs, transfer[0])
        upward = dot_narrow(middle, transfer[1])

        def place(ref, value, start=0):
            for slot, mask in enumerate(masks):
                rows = value[slot * part : (slot + 1) * part, :]
                ref[pl.ds(pl.multiple_of(start + (position ^ mask) * part, 16), part), :] = rows

        for msg, value, start in ((up_msg, upward, 0), (low_msg, coeffs, 0), (low_msg, middle, total + EXTRA)):
            scaled, power = encode(value)
            place(msg, scaled, start)
            msg[start + total : start + total + EXTRA, :] = power
        place(up_ref, upward)
        place(mid_ref, middle)

    plain = shape(total, rank)
    cols, up_msg, low_msg, upward, middle = call(
        leaf_body,
        (shape(total, leaf, dtype=BF16), message, shape(2 * (total + EXTRA), rank), plain, plain),
        (blocks[0], *came, basis, low),
        flops=2 * total * leaf * rank,
        moved=2**21,
        in_specs=[VMEM] * 6,
        out_specs=[VMEM] * 5,
    )
    up_msg, low_msg = up_msg.astype(F16), low_msg.astype(F16)
    ups = [swap(up_msg, "rhs", mask).astype(F32) for mask in masks[1:]]
    low_sib = swap(low_msg, "rhs", 1).astype(F32)

    def near_half(cols, half):
        width = leaf // 8

        def body(cols_ref, block_ref, out_ref):
            for step in range(4):
                rows = block_ref[0, (4 * half + step) * width : (4 * half + step + 1) * width, :]
                out_ref[:, step * width : (step + 1) * width] = lax.dot_general(
                    cols_ref[...], rows, (((1,), (1,)), ((), ())), preferred_element_type=F32
                )

        return call(
            body,
            shape(total, leaf // 2),
            (cols, near_blocks),
            flops=total * leaf * leaf,
            moved=leaf * leaf + 3 * total * leaf,
            in_specs=[VMEM] * 2,
            out_specs=VMEM,
        )

    near_left = near_half(cols, 0)
    ups, near_left = lax.optimization_barrier((ups, near_left))

    def group_body(own, a, b, c, out):
        out[...] = own[...] + decode(a) + (decode(b) + decode(c))

    group = call(
        group_body,
        plain,
        (upward, *ups),
        moved=2**20,
        in_specs=[VMEM] * 4,
        out_specs=VMEM,
    )
    group_sib = swap(group, "leaf", 1)

    def chip_body(own, sibling, matrices, mid_ref, low_ref, out, kept, cousin_msg):
        value = dot_narrow(own[...], matrices[:rank, :]) + dot_narrow(sibling[...], matrices[rank:, :])
        kept[...] = value
        put_encoded(out, value)
        put_encoded(cousin_msg, mid_ref[...] + decode(low_ref.at[total + EXTRA :, :]))

    chip_msg, chip, cousin_msg = call(
        chip_body,
        (message, plain, message),
        (group, group_sib, pair, middle, low_sib),
        flops=8 * total * rank * rank,
        moved=2**20,
        in_specs=[VMEM] * 5,
        out_specs=[VMEM] * 3,
    )
    chip_msg = chip_msg.astype(F16)
    chips, _ = line(chip_msg, "leaf", 2)
    chips = [got.astype(F32) for got in chips]

    cousin_msg = cousin_msg.astype(F16)
    cousin = swap(cousin_msg, "rhs", 3).astype(F32)

    def line_body(own, a, b, c, high, low, out):
        value = jnp.concatenate([own[...]] + [decode(ref) for ref in (a, b, c)], axis=1)
        put_encoded(out, dot_wide(value, high[...], low[...]))

    line_msg = call(
        line_body,
        message,
        (chip, *chips, up_high, up_low),
        flops=24 * total * rank * rank,
        moved=2**21,
        in_specs=[VMEM] * 6,
        out_specs=VMEM,
    )
    line_msg, cols = lax.optimization_barrier((line_msg.astype(F16), cols))
    def partial_body(sibling, others, core, z1, z2, z3, high, low, out):
        value = jnp.concatenate(
            [decode(sibling.at[: total + EXTRA, :]), decode(others), core[...]]
            + [decode(ref) for ref in (z1, z2, z3)],
            axis=1,
        )
        out[...] = dot_wide(value, high[...], low[...])

    partial = call(
        partial_body,
        plain,
        (low_sib, cousin, group_sib, *chips, acc_high, acc_low),
        flops=36 * total * rank * rank,
        moved=2**21,
        in_specs=[VMEM] * 8,
        out_specs=VMEM,
    )

    lines, _ = line(line_msg, "leaf", 8)
    lines = [got.astype(F32) for got in lines]
    near_right = near_half(cols, 1)

    out_masks = (0, 2, 1, 3)

    def last_body(part_ref, a, b, c, high, low, basis_ref, left, right, own, first, second, third, inner):
        position = lax.axis_index("rhs")
        value = jnp.concatenate([decode(ref) for ref in (a, b, c)], axis=1)
        inner[...] = part_ref[...] + dot_wide(value, high[...], low[...])
        coeffs = jnp.concatenate([inner[aligned(position ^ mask, part), :] for mask in masks], axis=0)
        far = lax.dot_general(
            coeffs.astype(BF16), basis_ref[...], (((1,), (1,)), ((), ())), preferred_element_type=F32
        )
        for mask, ref in zip(out_masks, (own, first, second, third)):
            slot = masks.index(mask)
            rows = slice(slot * part, (slot + 1) * part)
            ref[:, : leaf // 2] = (left[rows, :] + far[rows, : leaf // 2]).astype(ref.dtype)
            ref[:, leaf // 2 :] = (right[rows, :] + far[rows, leaf // 2 :]).astype(ref.dtype)

    sent = shape(part, leaf, dtype=BF16)
    own, *blocks = call(
        last_body,
        (shape(part, leaf), sent, sent, sent),
        (partial, *lines, top_high, top_low, basis, near_left, near_right),
        flops=2 * total * leaf * rank,
        moved=2**22,
        in_specs=[VMEM] * 9,
        out_specs=[VMEM] * 4,
        scratch_shapes=[pltpu.VMEM((total, rank), F32)],
    )
    blocks = [swap(block, "rhs", mask) for block, mask in zip(blocks, out_masks[1:])]

    def join_body(count, slots, *refs):
        blocks, out, wide, sems = refs[:count], refs[-3], refs[-2], refs[-1]
        position = lax.axis_index("rhs")
        copies = []
        for i, (block, slot) in enumerate(zip(blocks, slots)):
            wide[i] = block[...].astype(F32)
            target = out.at[:, aligned(position ^ out_masks[slot], leaf)]
            copies.append(pltpu.make_async_copy(wide.at[i], target, sems.at[i]))
            copies[-1].start()
        for copy in copies:
            copy.wait()

    def join(blocks, slots, under=None):
        count = len(blocks)

        def body(*refs):
            join_body(count, slots, *refs)

        return call(
            body,
            shape(part, 4 * leaf),
            (*blocks,) if under is None else (*blocks, under),
            moved=6 * part * leaf * count,
            in_specs=[VMEM] * count + ([] if under is None else [HBM]),
            out_specs=HBM,
            scratch_shapes=[pltpu.VMEM((count, part, leaf), F32), pltpu.SemaphoreType.DMA((count,))],
            input_output_aliases={} if under is None else {count: 0},
        )

    most = join((own, blocks[0], blocks[1]), (0, 1, 2))
    return join((blocks[2],), (3,), most)


def solution(mesh):
    in_specs = (
        P("rhs", "leaf"),
        P(("leaf", "rhs"), None, None),
        P(("leaf", "rhs"), None, None),
        P(("leaf", "rhs"), None, None, None),
        P(("leaf", "rhs"), None, None, None),
        P(),
        P(),
    )
    out_specs = P("rhs", "leaf")
    return jax.shard_map(shards, mesh=mesh, in_specs=in_specs, out_specs=out_specs, check_vma=False)
```

```python
import jax
import jax.numpy as jnp
from jax import lax
from jax.experimental import pallas as pl
from jax.experimental.pallas import tpu as pltpu
from jax.sharding import PartitionSpec as P

F32 = jnp.float32
BF16 = jnp.bfloat16
F16 = jnp.float16
VMEM = pl.BlockSpec(memory_space=pltpu.VMEM)
HBM = pl.BlockSpec(memory_space=pltpu.HBM)
LIMIT = 32 * 2**20
EXTRA = 16


def swap(value, axis, mask):
    pairs = [(source, source ^ mask) for source in range(lax.axis_size(axis))]
    return lax.ppermute(value, axis, pairs)


def split(value):
    high = value.astype(BF16)
    return high, (value - high.astype(F32)).astype(BF16)


def dot(a, b):
    return jnp.dot(a, b, preferred_element_type=F32)


def dot_narrow(value, matrix):
    rows = value.shape[0]
    both = dot(jnp.concatenate(split(value), axis=0), matrix)
    return both[:rows] + both[rows:]


def dot_wide(value, high_matrix, low_matrix):
    return dot_narrow(value, high_matrix) + dot(value.astype(BF16), low_matrix)


def encode(value):
    largest = jnp.max(jnp.abs(value), axis=0, keepdims=True)
    power = jnp.ceil(jnp.log2(jnp.maximum(largest, 1e-30))) - 14.0
    scaled = value * jnp.exp2(-power)
    return scaled, jnp.broadcast_to(power, (EXTRA, value.shape[1]))


def put_encoded(ref, value):
    rows = value.shape[0]
    ref[:rows, :], ref[rows:, :] = encode(value)


def decode(ref):
    rows = ref.shape[0] - EXTRA
    return ref[:rows, :] * jnp.exp2(ref[rows : rows + 1, :])


def call(body, outs, operands, flops=0, moved=0, **more):
    return pl.pallas_call(
        body,
        out_shape=outs,
        compiler_params=pltpu.CompilerParams(vmem_limit_bytes=LIMIT),
        cost_estimate=pl.CostEstimate(flops=flops, bytes_accessed=moved, transcendentals=0),
        **more,
    )(*operands)


def shape(*dims, dtype=F32):
    return jax.ShapeDtypeStruct(dims, dtype)


def line(message, axis, step, beside=None):
    leaves, group = lax.axis_size("leaf"), lax.axis_size("rhs")
    if axis == "leaf":
        pairs = [(i, i ^ step * (1 + (i & 1))) for i in range(leaves)]
    else:
        axis = ("leaf", "rhs")
        pairs = [(i * group + j, i * group + (j ^ (1 + (i & 1)))) for i in range(leaves) for j in range(group)]
    mine = lax.ppermute(message, axis, pairs)
    third = swap(message, "leaf" if axis == "leaf" else "rhs", 3 * step)
    if beside is not None:
        mine, beside = lax.optimization_barrier((mine, beside))
    return [mine, swap(mine, "leaf", 1), third], beside


def aligned(index, size):
    return pl.ds(pl.multiple_of(index * size, size), size)


def cut(vectors, leaf, masks):
    part = vectors.shape[0]

    def body(source, *rest):
        blocks, sems = rest[:-1], rest[-1]
        position = lax.axis_index("rhs")
        copies = [
            pltpu.make_async_copy(source.at[:, aligned(position ^ mask, leaf)], block, sems.at[slot])
            for slot, (mask, block) in enumerate(zip(masks, blocks))
        ]
        for copy in copies:
            copy.start()
        for copy in copies:
            copy.wait()

    count = len(masks)
    return call(
        body,
        [shape(part, leaf, dtype=BF16)] * count,
        (vectors,),
        moved=4 * count * part * leaf,
        in_specs=[HBM],
        out_specs=[VMEM] * count,
        scratch_shapes=[pltpu.SemaphoreType.DMA((count,))],
    )


def oriented(coupling, is_right):
    wide = coupling.astype(F32)
    return jnp.where(is_right == 1, wide, wide.T).astype(BF16)


def transposed(matrix):
    return matrix.astype(F32).T.astype(BF16)


def times(matrix, parts):
    return dot(matrix, parts[0]) + dot(matrix, parts[1])


PICKS = [(0, 0), (0, 1), (1, 0), (1, 1), (1, 2), (1, 3), (2, 0), (2, 1), (3, 0), (3, 2), (3, 3)]
COUPLED = 5


def compose(leaf_basis, lower_transfer, lower_coupling, upper_transfer, upper_coupling):
    leaf, rank = leaf_basis.shape[1:]
    n_up = len(PICKS)
    n_all = n_up + COUPLED

    def body(basis_hbm, low_t_hbm, low_b_hbm, up_t_hbm, up_b_hbm, *rest):
        basis, lower_t, lower_down, coupled, pair, up_high, up_low, acc_high, acc_low, top_high, top_low = rest[:11]
        lower_b, uppers, couplings, sems = rest[11:]
        rhs_pos = lax.axis_index("rhs")
        node = lax.axis_index("leaf") + lax.axis_size("leaf")
        copies = {}

        def start(name, source, target):
            copies[name] = pltpu.make_async_copy(source, target, sems.at[len(copies)])
            copies[name].start()

        start("t", low_t_hbm.at[0], lower_t)
        start("b", low_b_hbm.at[0], lower_b)
        for slot, (height, mask) in enumerate(PICKS):
            start(slot, up_t_hbm.at[((node >> height) ^ mask) - 2], uppers.at[slot])
        for height in range(COUPLED):
            start(n_up + height, up_b_hbm.at[(node >> (height + 1)) - 1], couplings.at[height])
        start("basis", basis_hbm.at[0], basis)

        def upper(slot):
            copies[slot].wait()
            return uppers[slot]

        def coupling(height):
            copies[n_up + height].wait()
            return couplings[height]

        def put(high_ref, low_ref, slot, value):
            high, low = split(value)
            high_ref[aligned(slot, rank), :] = high
            low_ref[aligned(slot, rank), :] = low

        first = node & 1
        second = 1 - first

        copies["t"].wait()
        copies["b"].wait()
        for level in range(2):
            coupled[level] = oriented(lower_b[level], rhs_pos >> level & 1)
            lower_down[level] = transposed(lower_t[level])
        own2 = upper(0)
        pair[:rank, :] = own2
        pair[rank:, :] = upper(1)
        level3 = [upper(slot) for slot in range(2, 6)]
        own4, sib4, own5, third5, fourth5 = [upper(slot) for slot in range(6, 11)]
        coupled[2] = oriented(coupling(0), node & 1)
        down = transposed(own2)
        put(acc_high, acc_low, first, dot(oriented(coupling(1), node >> 1 & 1), down))
        down = split(dot(transposed(level3[0]), down))
        across = split(times(oriented(coupling(2), node >> 2 & 1), down))
        put(acc_high, acc_low, second, times(level3[2], across))
        put(acc_high, acc_low, 2, times(level3[3], across))
        down = split(times(transposed(own4), down))
        put(top_high, top_low, first, times(oriented(coupling(3), node >> 3 & 1), down))
        down = split(times(transposed(own5), down))
        across = split(times(oriented(coupling(4), node >> 4 & 1), down))
        put(top_high, top_low, second, times(third5, across))
        put(top_high, top_low, 2, times(fourth5, across))
        put(up_high, up_low, 0, dot(level3[0], own4))
        put(up_high, up_low, 1 + first, dot(level3[1], own4))
        put(up_high, up_low, 1 + second, dot(level3[2], sib4))
        put(up_high, up_low, 3, dot(level3[3], sib4))
        copies["basis"].wait()

    stacked = [shape(n * rank, rank, dtype=BF16) for n in (2, 4, 4, 3, 3, 3, 3)]
    lower = shape(2, rank, rank, dtype=BF16)
    return call(
        body,
        [shape(leaf, rank, dtype=BF16), lower, lower, shape(3, rank, rank, dtype=BF16)] + stacked,
        (leaf_basis, lower_transfer, lower_coupling, upper_transfer, upper_coupling),
        flops=34 * 2 * rank**3,
        moved=2**22,
        in_specs=[HBM] * 5,
        out_specs=[VMEM] * 11,
        scratch_shapes=[
            pltpu.VMEM((2, rank, rank), BF16),
            pltpu.VMEM((n_up, rank, rank), BF16),
            pltpu.VMEM((COUPLED, rank, rank), BF16),
            pltpu.SemaphoreType.DMA((n_all + 3,)),
        ],
    )


def shards(
    vectors, near_blocks, leaf_basis, lower_transfer, lower_coupling, upper_transfer, upper_coupling
):
    part = vectors.shape[0]
    leaf, rank = leaf_basis.shape[1:]
    total = part * lax.axis_size("rhs")
    masks = (0, 1, 3, 2)

    vectors = pltpu.with_memory_space_constraint(vectors, pltpu.HBM)
    blocks = cut(vectors, leaf, masks)
    came = [swap(block, "rhs", mask) for block, mask in zip(blocks[1:], masks[1:])]
    leaf_basis, lower_transfer, lower_coupling, upper_transfer, upper_coupling = [
        pltpu.with_memory_space_constraint(array, pltpu.HBM)
        for array in (leaf_basis, lower_transfer, lower_coupling, upper_transfer, upper_coupling)
    ]
    basis, low, low_down, coupled, pair, up_high, up_low, acc_high, acc_low, top_high, top_low = compose(
        leaf_basis, lower_transfer, lower_coupling, upper_transfer, upper_coupling
    )
    message = shape(total + EXTRA, rank)

    def place(ref, value):
        position = lax.axis_index("rhs")
        for slot, mask in enumerate(masks):
            ref[aligned(position ^ mask, part), :] = value[slot * part : (slot + 1) * part, :]

    def leaf_body(own, first, second, third, basis_ref, transfer, cols, up_msg, coeff_ref, mid_ref, up_ref):
        for slot, ref in enumerate((own, first, second, third)):
            cols[slot * part : (slot + 1) * part, :] = ref[...]
        coeffs = dot(cols[...], basis_ref[...])
        place(coeff_ref, coeffs)
        middle = dot_narrow(coeffs, transfer[0])
        place(mid_ref, middle)
        upward = dot_narrow(middle, transfer[1])
        place(up_ref, upward)
        scaled, power = encode(upward)
        place(up_msg, scaled)
        up_msg[total:, :] = power

    plain = shape(total, rank)
    cols, up_msg, coeffs, middle, upward = call(
        leaf_body,
        (shape(total, leaf, dtype=BF16), message, plain, plain, plain),
        (blocks[0], *came, basis, low),
        flops=2 * total * leaf * rank,
        moved=2**21,
        in_specs=[VMEM] * 6,
        out_specs=[VMEM] * 5,
    )
    up_msg = up_msg.astype(F16)
    ups = [swap(up_msg, "rhs", mask).astype(F32) for mask in masks[1:]]

    def low_body(coeff_ref, mid_ref, low_msg):
        put_encoded(low_msg.at[: total + EXTRA, :], coeff_ref[...])
        put_encoded(low_msg.at[total + EXTRA :, :], mid_ref[...])

    low_msg = call(
        low_body,
        shape(2 * (total + EXTRA), rank),
        (coeffs, middle),
        moved=2**20,
        in_specs=[VMEM] * 2,
        out_specs=VMEM,
    )
    low_sib = swap(low_msg.astype(F16), "rhs", 1).astype(F32)

    def near_half(cols, half):
        width = leaf // 8

        def body(cols_ref, block_ref, out_ref):
            for step in range(4):
                rows = block_ref[0, (4 * half + step) * width : (4 * half + step + 1) * width, :]
                out_ref[:, step * width : (step + 1) * width] = lax.dot_general(
                    cols_ref[...], rows, (((1,), (1,)), ((), ())), preferred_element_type=F32
                )

        return call(
            body,
            shape(total, leaf // 2),
            (cols, near_blocks),
            flops=total * leaf * leaf,
            moved=leaf * leaf + 3 * total * leaf,
            in_specs=[VMEM] * 2,
            out_specs=VMEM,
        )

    def flip_body(basis_ref, out):
        for step in range(8):
            rows = slice(step * leaf // 8, (step + 1) * leaf // 8)
            out[:, rows] = basis_ref[rows, :].astype(F32).T.astype(BF16)

    flipped = call(
        flip_body,
        shape(rank, leaf, dtype=BF16),
        (basis,),
        moved=2**21,
        in_specs=[VMEM],
        out_specs=VMEM,
    )
    near_left = near_half(cols, 0)
    ups, near_left, flipped = lax.optimization_barrier((ups, near_left, flipped))

    def group_body(own, a, b, c, out):
        out[...] = own[...] + decode(a) + (decode(b) + decode(c))

    group = call(
        group_body,
        plain,
        (upward, *ups),
        moved=2**20,
        in_specs=[VMEM] * 4,
        out_specs=VMEM,
    )
    group_sib = swap(group, "leaf", 1)

    def chip_body(own, sibling, matrices, mid_ref, low_ref, out, kept, cousin_msg):
        value = dot_narrow(own[...], matrices[:rank, :]) + dot_narrow(sibling[...], matrices[rank:, :])
        kept[...] = value
        put_encoded(out, value)
        put_encoded(cousin_msg, mid_ref[...] + decode(low_ref.at[total + EXTRA :, :]))

    chip_msg, chip, cousin_msg = call(
        chip_body,
        (message, plain, message),
        (group, group_sib, pair, middle, low_sib),
        flops=8 * total * rank * rank,
        moved=2**20,
        in_specs=[VMEM] * 5,
        out_specs=[VMEM] * 3,
    )
    chip_msg = chip_msg.astype(F16)
    chips, _ = line(chip_msg, "leaf", 2)
    chips = [got.astype(F32) for got in chips]

    cousin_msg = cousin_msg.astype(F16)
    cousin = swap(cousin_msg, "rhs", 3).astype(F32)

    def line_body(own, a, b, c, high, low, out):
        value = jnp.concatenate([own[...]] + [decode(ref) for ref in (a, b, c)], axis=1)
        put_encoded(out, dot_wide(value, high[...], low[...]))

    line_msg = call(
        line_body,
        message,
        (chip, *chips, up_high, up_low),
        flops=24 * total * rank * rank,
        moved=2**21,
        in_specs=[VMEM] * 6,
        out_specs=VMEM,
    )
    line_msg, cols = lax.optimization_barrier((line_msg.astype(F16), cols))
    def partial_body(sibling, others, core, z1, z2, z3, pairs, high, low, at_leaf, at_pair, at_group):
        at_leaf[...] = dot_narrow(decode(sibling.at[: total + EXTRA, :]), pairs[0])
        at_pair[...] = dot_narrow(decode(others), pairs[1])
        value = jnp.concatenate([decode(ref) for ref in (z1, z2, z3)], axis=1)
        at_group[...] = dot_narrow(core[...], pairs[2]) + dot_wide(value, high[...], low[...])

    partials = call(
        partial_body,
        (plain, plain, plain),
        (low_sib, cousin, group_sib, *chips, coupled, acc_high, acc_low),
        flops=36 * total * rank * rank,
        moved=2**21,
        in_specs=[VMEM] * 9,
        out_specs=[VMEM] * 3,
    )
    lines, _ = line(line_msg, "leaf", 8)
    lines = [got.astype(F32) for got in lines]
    near_right = near_half(cols, 1)

    out_masks = (0, 2, 1, 3)

    def last_body(at_leaf, at_pair, at_group, a, b, c, high, low, steps, basis_ref, left, right, own, first, second, third, inner):
        position = lax.axis_index("rhs")
        value = jnp.concatenate([decode(ref) for ref in (a, b, c)], axis=1)
        value = at_group[...] + dot_wide(value, high[...], low[...])
        value = at_pair[...] + dot_narrow(value, steps[1])
        inner[...] = at_leaf[...] + dot_narrow(value, steps[0])
        coeffs = jnp.concatenate([inner[aligned(position ^ mask, part), :] for mask in masks], axis=0)
        far = dot(coeffs.astype(BF16), basis_ref[...])
        for mask, ref in zip(out_masks, (own, first, second, third)):
            slot = masks.index(mask)
            rows = slice(slot * part, (slot + 1) * part)
            ref[:, : leaf // 2] = (left[rows, :] + far[rows, : leaf // 2]).astype(ref.dtype)
            ref[:, leaf // 2 :] = (right[rows, :] + far[rows, leaf // 2 :]).astype(ref.dtype)

    sent = shape(part, leaf, dtype=BF16)
    own, *blocks = call(
        last_body,
        (shape(part, leaf), sent, sent, sent),
        (*partials, *lines, top_high, top_low, low_down, flipped, near_left, near_right),
        flops=2 * total * leaf * rank,
        moved=2**22,
        in_specs=[VMEM] * 12,
        out_specs=[VMEM] * 4,
        scratch_shapes=[pltpu.VMEM((total, rank), F32)],
    )
    blocks = [swap(block, "rhs", mask) for block, mask in zip(blocks, out_masks[1:])]

    def join_body(count, slots, *refs):
        blocks, out, wide, sems = refs[:count], refs[-3], refs[-2], refs[-1]
        position = lax.axis_index("rhs")
        copies = []
        for i, (block, slot) in enumerate(zip(blocks, slots)):
            wide[i] = block[...].astype(F32)
            target = out.at[:, aligned(position ^ out_masks[slot], leaf)]
            copies.append(pltpu.make_async_copy(wide.at[i], target, sems.at[i]))
            copies[-1].start()
        for copy in copies:
            copy.wait()

    def join(blocks, slots, under=None):
        count = len(blocks)

        def body(*refs):
            join_body(count, slots, *refs)

        return call(
            body,
            shape(part, 4 * leaf),
            (*blocks,) if under is None else (*blocks, under),
            moved=6 * part * leaf * count,
            in_specs=[VMEM] * count + ([] if under is None else [HBM]),
            out_specs=HBM,
            scratch_shapes=[pltpu.VMEM((count, part, leaf), F32), pltpu.SemaphoreType.DMA((count,))],
            input_output_aliases={} if under is None else {count: 0},
        )

    most = join((own, blocks[0]), (0, 1))
    return join(blocks[1:], (2, 3), most)


def solution(mesh):
    in_specs = (
        P("rhs", "leaf"),
        P(("leaf", "rhs"), None, None),
        P(("leaf", "rhs"), None, None),
        P(("leaf", "rhs"), None, None, None),
        P(("leaf", "rhs"), None, None, None),
        P(),
        P(),
    )
    out_specs = P("rhs", "leaf")
    return jax.shard_map(shards, mesh=mesh, in_specs=in_specs, out_specs=out_specs, check_vma=False)
```

```python
import jax
import jax.numpy as jnp
from jax import lax
from jax.experimental import pallas as pl
from jax.experimental.pallas import tpu as pltpu
from jax.sharding import PartitionSpec as P

F32 = jnp.float32
BF16 = jnp.bfloat16
F16 = jnp.float16
VMEM = pl.BlockSpec(memory_space=pltpu.VMEM)
HBM = pl.BlockSpec(memory_space=pltpu.HBM)
LIMIT = 32 * 2**20
EXTRA = 16


def swap(value, axis, mask):
    pairs = [(source, source ^ mask) for source in range(lax.axis_size(axis))]
    return lax.ppermute(value, axis, pairs)


def split(value):
    high = value.astype(BF16)
    return high, (value - high.astype(F32)).astype(BF16)


def dot(a, b):
    return jnp.dot(a, b, preferred_element_type=F32)


def dot_narrow(value, matrix):
    rows = value.shape[0]
    both = dot(jnp.concatenate(split(value), axis=0), matrix)
    return both[:rows] + both[rows:]


def dot_wide(value, high_matrix, low_matrix):
    return dot_narrow(value, high_matrix) + dot(value.astype(BF16), low_matrix)


def encode(value):
    largest = jnp.max(jnp.abs(value), axis=0, keepdims=True)
    power = jnp.ceil(jnp.log2(jnp.maximum(largest, 1e-30))) - 14.0
    scaled = value * jnp.exp2(-power)
    return scaled, jnp.broadcast_to(power, (EXTRA, value.shape[1]))


def put_encoded(ref, value):
    rows = value.shape[0]
    ref[:rows, :], ref[rows:, :] = encode(value)


def decode(ref):
    rows = ref.shape[0] - EXTRA
    return ref[:rows, :] * jnp.exp2(ref[rows : rows + 1, :])


def call(body, outs, operands, flops=0, moved=0, **more):
    return pl.pallas_call(
        body,
        out_shape=outs,
        compiler_params=pltpu.CompilerParams(vmem_limit_bytes=LIMIT),
        cost_estimate=pl.CostEstimate(flops=flops, bytes_accessed=moved, transcendentals=0),
        **more,
    )(*operands)


def shape(*dims, dtype=F32):
    return jax.ShapeDtypeStruct(dims, dtype)


def line(message, axis, step, beside=None):
    leaves, group = lax.axis_size("leaf"), lax.axis_size("rhs")
    if axis == "leaf":
        pairs = [(i, i ^ step * (1 + (i & 1))) for i in range(leaves)]
    else:
        axis = ("leaf", "rhs")
        pairs = [(i * group + j, i * group + (j ^ (1 + (i & 1)))) for i in range(leaves) for j in range(group)]
    mine = lax.ppermute(message, axis, pairs)
    third = swap(message, "leaf" if axis == "leaf" else "rhs", 3 * step)
    if beside is not None:
        mine, beside = lax.optimization_barrier((mine, beside))
    return [mine, swap(mine, "leaf", 1), third], beside


def aligned(index, size):
    return pl.ds(pl.multiple_of(index * size, size), size)


def cut(vectors, leaf, masks):
    part = vectors.shape[0]

    def body(source, *rest):
        blocks, sems = rest[:-1], rest[-1]
        position = lax.axis_index("rhs")
        half = part // 2
        copies = [
            pltpu.make_async_copy(
                source.at[rows, aligned(position ^ mask, leaf)], block.at[rows, :], sems.at[2 * slot + side]
            )
            for slot, (mask, block) in enumerate(zip(masks, blocks))
            for side, rows in enumerate((slice(0, half), slice(half, part)))
        ]
        for copy in copies:
            copy.start()
        for copy in copies:
            copy.wait()

    count = len(masks)
    return call(
        body,
        [shape(part, leaf, dtype=BF16)] * count,
        (vectors,),
        moved=4 * count * part * leaf,
        in_specs=[HBM],
        out_specs=[VMEM] * count,
        scratch_shapes=[pltpu.SemaphoreType.DMA((2 * count,))],
    )


def oriented(coupling, is_right):
    wide = coupling.astype(F32)
    return jnp.where(is_right == 1, wide, wide.T).astype(BF16)


def transposed(matrix):
    return matrix.astype(F32).T.astype(BF16)


def times(matrix, parts):
    return dot(matrix, parts[0]) + dot(matrix, parts[1])


PICKS = [(0, 0), (0, 1), (1, 0), (1, 1), (1, 2), (1, 3), (2, 0), (2, 1), (3, 0), (3, 2), (3, 3)]
COUPLED = 5


def compose(vectors, leaf_basis, lower_transfer, lower_coupling, upper_transfer, upper_coupling):
    leaf, rank = leaf_basis.shape[1:]
    n_up = len(PICKS)
    n_all = n_up + COUPLED

    def body(vectors_hbm, basis_hbm, low_t_hbm, low_b_hbm, up_t_hbm, up_b_hbm, *rest):
        own_block, basis, lower_t, lower_down, coupled, pair, up_high, up_low, acc_high, acc_low, top_high, top_low = rest[:12]
        lower_b, uppers, couplings, sems = rest[12:]
        rhs_pos = lax.axis_index("rhs")
        node = lax.axis_index("leaf") + lax.axis_size("leaf")
        copies = {}

        def start(name, source, target):
            copies[name] = pltpu.make_async_copy(source, target, sems.at[len(copies)])
            copies[name].start()

        start("t", low_t_hbm.at[0], lower_t)
        start("b", low_b_hbm.at[0], lower_b)
        for slot, (height, mask) in enumerate(PICKS):
            start(slot, up_t_hbm.at[((node >> height) ^ mask) - 2], uppers.at[slot])
        for height in range(COUPLED):
            start(n_up + height, up_b_hbm.at[(node >> (height + 1)) - 1], couplings.at[height])
        start("basis", basis_hbm.at[0], basis)
        start("own", vectors_hbm.at[:, aligned(rhs_pos, leaf)], own_block)

        def upper(slot):
            copies[slot].wait()
            return uppers[slot]

        def coupling(height):
            copies[n_up + height].wait()
            return couplings[height]

        def put(high_ref, low_ref, slot, value):
            high, low = split(value)
            high_ref[aligned(slot, rank), :] = high
            low_ref[aligned(slot, rank), :] = low

        first = node & 1
        second = 1 - first

        copies["t"].wait()
        copies["b"].wait()
        for level in range(2):
            coupled[level] = oriented(lower_b[level], rhs_pos >> level & 1)
            lower_down[level] = transposed(lower_t[level])
        own2 = upper(0)
        pair[:rank, :] = own2
        pair[rank:, :] = upper(1)
        level3 = [upper(slot) for slot in range(2, 6)]
        own4, sib4, own5, third5, fourth5 = [upper(slot) for slot in range(6, 11)]
        coupled[2] = oriented(coupling(0), node & 1)
        down = transposed(own2)
        put(acc_high, acc_low, first, dot(oriented(coupling(1), node >> 1 & 1), down))
        down = split(dot(transposed(level3[0]), down))
        across = split(times(oriented(coupling(2), node >> 2 & 1), down))
        put(acc_high, acc_low, second, times(level3[2], across))
        put(acc_high, acc_low, 2, times(level3[3], across))
        down = split(times(transposed(own4), down))
        put(top_high, top_low, first, times(oriented(coupling(3), node >> 3 & 1), down))
        down = split(times(transposed(own5), down))
        across = split(times(oriented(coupling(4), node >> 4 & 1), down))
        put(top_high, top_low, second, times(third5, across))
        put(top_high, top_low, 2, times(fourth5, across))
        put(up_high, up_low, 0, dot(level3[0], own4))
        put(up_high, up_low, 1 + first, dot(level3[1], own4))
        put(up_high, up_low, 1 + second, dot(level3[2], sib4))
        put(up_high, up_low, 3, dot(level3[3], sib4))
        copies["basis"].wait()
        copies["own"].wait()

    stacked = [shape(n * rank, rank, dtype=BF16) for n in (2, 4, 4, 3, 3, 3, 3)]
    lower = shape(2, rank, rank, dtype=BF16)
    return call(
        body,
        [shape(vectors.shape[0], leaf, dtype=BF16), shape(leaf, rank, dtype=BF16), lower, lower, shape(3, rank, rank, dtype=BF16)] + stacked,
        (vectors, leaf_basis, lower_transfer, lower_coupling, upper_transfer, upper_coupling),
        flops=34 * 2 * rank**3,
        moved=2**22,
        in_specs=[HBM] * 6,
        out_specs=[VMEM] * 12,
        scratch_shapes=[
            pltpu.VMEM((2, rank, rank), BF16),
            pltpu.VMEM((n_up, rank, rank), BF16),
            pltpu.VMEM((COUPLED, rank, rank), BF16),
            pltpu.SemaphoreType.DMA((n_all + 4,)),
        ],
    )


def shards(
    vectors, near_blocks, leaf_basis, lower_transfer, lower_coupling, upper_transfer, upper_coupling
):
    part = vectors.shape[0]
    leaf, rank = leaf_basis.shape[1:]
    total = part * lax.axis_size("rhs")
    masks = (0, 1, 3, 2)

    vectors = pltpu.with_memory_space_constraint(vectors, pltpu.HBM)
    blocks = cut(vectors, leaf, masks[1:])
    came = [swap(block, "rhs", mask) for block, mask in zip(blocks, masks[1:])]
    leaf_basis, lower_transfer, lower_coupling, upper_transfer, upper_coupling = [
        pltpu.with_memory_space_constraint(array, pltpu.HBM)
        for array in (leaf_basis, lower_transfer, lower_coupling, upper_transfer, upper_coupling)
    ]
    own_block, basis, low, low_down, coupled, pair, up_high, up_low, acc_high, acc_low, top_high, top_low = compose(
        vectors, leaf_basis, lower_transfer, lower_coupling, upper_transfer, upper_coupling
    )
    message = shape(total + EXTRA, rank)

    def place(ref, value):
        position = lax.axis_index("rhs")
        for slot, mask in enumerate(masks):
            ref[aligned(position ^ mask, part), :] = value[slot * part : (slot + 1) * part, :]

    def leaf_body(own, first, second, third, basis_ref, transfer, cols, up_msg, coeff_ref, mid_ref, up_ref):
        for slot, ref in enumerate((own, first, second, third)):
            cols[slot * part : (slot + 1) * part, :] = ref[...]
        coeffs = dot(cols[...], basis_ref[...])
        place(coeff_ref, coeffs)
        middle = dot_narrow(coeffs, transfer[0])
        place(mid_ref, middle)
        upward = dot_narrow(middle, transfer[1])
        place(up_ref, upward)
        scaled, power = encode(upward)
        place(up_msg, scaled)
        up_msg[total:, :] = power

    plain = shape(total, rank)
    cols, up_msg, coeffs, middle, upward = call(
        leaf_body,
        (shape(total, leaf, dtype=BF16), message, plain, plain, plain),
        (own_block, *came, basis, low),
        flops=2 * total * leaf * rank,
        moved=2**21,
        in_specs=[VMEM] * 6,
        out_specs=[VMEM] * 5,
    )
    up_msg = up_msg.astype(F16)
    ups = [swap(up_msg, "rhs", mask).astype(F32) for mask in masks[1:]]

    def low_body(coeff_ref, mid_ref, low_msg):
        put_encoded(low_msg.at[: total + EXTRA, :], coeff_ref[...])
        put_encoded(low_msg.at[total + EXTRA :, :], mid_ref[...])

    low_msg = call(
        low_body,
        shape(2 * (total + EXTRA), rank),
        (coeffs, middle),
        moved=2**20,
        in_specs=[VMEM] * 2,
        out_specs=VMEM,
    )
    low_sib = swap(low_msg.astype(F16), "rhs", 1).astype(F32)

    def near_half(cols, half):
        width = leaf // 8

        def body(cols_ref, block_ref, out_ref):
            for step in range(4):
                rows = block_ref[0, (4 * half + step) * width : (4 * half + step + 1) * width, :]
                out_ref[:, step * width : (step + 1) * width] = lax.dot_general(
                    cols_ref[...], rows, (((1,), (1,)), ((), ())), preferred_element_type=F32
                )

        return call(
            body,
            shape(total, leaf // 2),
            (cols, near_blocks),
            flops=total * leaf * leaf,
            moved=leaf * leaf + 3 * total * leaf,
            in_specs=[VMEM] * 2,
            out_specs=VMEM,
        )

    def flip_body(basis_ref, out):
        for step in range(8):
            rows = slice(step * leaf // 8, (step + 1) * leaf // 8)
            out[:, rows] = basis_ref[rows, :].astype(F32).T.astype(BF16)

    flipped = call(
        flip_body,
        shape(rank, leaf, dtype=BF16),
        (basis,),
        moved=2**21,
        in_specs=[VMEM],
        out_specs=VMEM,
    )
    near_left = near_half(cols, 0)
    ups, near_left, flipped = lax.optimization_barrier((ups, near_left, flipped))

    def group_body(own, a, b, c, out):
        out[...] = own[...] + decode(a) + (decode(b) + decode(c))

    group = call(
        group_body,
        plain,
        (upward, *ups),
        moved=2**20,
        in_specs=[VMEM] * 4,
        out_specs=VMEM,
    )
    group_sib = swap(group, "leaf", 1)

    def chip_body(own, sibling, matrices, mid_ref, low_ref, out, kept, cousin_msg):
        value = dot_narrow(own[...], matrices[:rank, :]) + dot_narrow(sibling[...], matrices[rank:, :])
        kept[...] = value
        put_encoded(out, value)
        put_encoded(cousin_msg, mid_ref[...] + decode(low_ref.at[total + EXTRA :, :]))

    chip_msg, chip, cousin_msg = call(
        chip_body,
        (message, plain, message),
        (group, group_sib, pair, middle, low_sib),
        flops=8 * total * rank * rank,
        moved=2**20,
        in_specs=[VMEM] * 5,
        out_specs=[VMEM] * 3,
    )
    chip_msg = chip_msg.astype(F16)
    chips, _ = line(chip_msg, "leaf", 2)
    chips = [got.astype(F32) for got in chips]

    cousin_msg = cousin_msg.astype(F16)
    cousin = swap(cousin_msg, "rhs", 3).astype(F32)

    def line_body(own, a, b, c, high, low, out):
        value = jnp.concatenate([own[...]] + [decode(ref) for ref in (a, b, c)], axis=1)
        put_encoded(out, dot_wide(value, high[...], low[...]))

    line_msg = call(
        line_body,
        message,
        (chip, *chips, up_high, up_low),
        flops=24 * total * rank * rank,
        moved=2**21,
        in_specs=[VMEM] * 6,
        out_specs=VMEM,
    )
    line_msg, cols = lax.optimization_barrier((line_msg.astype(F16), cols))
    def partial_body(sibling, others, core, z1, z2, z3, pairs, high, low, at_leaf, at_pair, at_group):
        at_leaf[...] = dot_narrow(decode(sibling.at[: total + EXTRA, :]), pairs[0])
        at_pair[...] = dot_narrow(decode(others), pairs[1])
        value = jnp.concatenate([decode(ref) for ref in (z1, z2, z3)], axis=1)
        at_group[...] = dot_narrow(core[...], pairs[2]) + dot_wide(value, high[...], low[...])

    partials = call(
        partial_body,
        (plain, plain, plain),
        (low_sib, cousin, group_sib, *chips, coupled, acc_high, acc_low),
        flops=36 * total * rank * rank,
        moved=2**21,
        in_specs=[VMEM] * 9,
        out_specs=[VMEM] * 3,
    )
    lines, _ = line(line_msg, "leaf", 8)
    lines = [got.astype(F32) for got in lines]
    near_right = near_half(cols, 1)

    out_masks = (0, 2, 1, 3)

    def last_body(at_leaf, at_pair, at_group, a, b, c, high, low, steps, basis_ref, left, right, own, first, second, third, inner):
        position = lax.axis_index("rhs")
        value = jnp.concatenate([decode(ref) for ref in (a, b, c)], axis=1)
        value = at_group[...] + dot_wide(value, high[...], low[...])
        value = at_pair[...] + dot_narrow(value, steps[1])
        inner[...] = at_leaf[...] + dot_narrow(value, steps[0])
        coeffs = jnp.concatenate([inner[aligned(position ^ mask, part), :] for mask in masks], axis=0)
        far = dot(coeffs.astype(BF16), basis_ref[...])
        for mask, ref in zip(out_masks, (own, first, second, third)):
            slot = masks.index(mask)
            rows = slice(slot * part, (slot + 1) * part)
            ref[:, : leaf // 2] = (left[rows, :] + far[rows, : leaf // 2]).astype(ref.dtype)
            ref[:, leaf // 2 :] = (right[rows, :] + far[rows, leaf // 2 :]).astype(ref.dtype)

    sent = shape(part, leaf, dtype=BF16)
    own, *blocks = call(
        last_body,
        (shape(part, leaf), sent, sent, sent),
        (*partials, *lines, top_high, top_low, low_down, flipped, near_left, near_right),
        flops=2 * total * leaf * rank,
        moved=2**22,
        in_specs=[VMEM] * 12,
        out_specs=[VMEM] * 4,
        scratch_shapes=[pltpu.VMEM((total, rank), F32)],
    )
    blocks = [swap(block, "rhs", mask) for block, mask in zip(blocks, out_masks[1:])]

    def join_body(count, slots, *refs):
        blocks, out, wide, sems = refs[:count], refs[-3], refs[-2], refs[-1]
        position = lax.axis_index("rhs")
        copies = []
        for i, (block, slot) in enumerate(zip(blocks, slots)):
            wide[i] = block[...].astype(F32)
            target = out.at[:, aligned(position ^ out_masks[slot], leaf)]
            copies.append(pltpu.make_async_copy(wide.at[i], target, sems.at[i]))
            copies[-1].start()
        for copy in copies:
            copy.wait()

    def join(blocks, slots, under=None):
        count = len(blocks)

        def body(*refs):
            join_body(count, slots, *refs)

        return call(
            body,
            shape(part, 4 * leaf),
            (*blocks,) if under is None else (*blocks, under),
            moved=6 * part * leaf * count,
            in_specs=[VMEM] * count + ([] if under is None else [HBM]),
            out_specs=HBM,
            scratch_shapes=[pltpu.VMEM((count, part, leaf), F32), pltpu.SemaphoreType.DMA((count,))],
            input_output_aliases={} if under is None else {count: 0},
        )

    most = join((own, blocks[0]), (0, 1))
    return join(blocks[1:], (2, 3), most)


def solution(mesh):
    in_specs = (
        P("rhs", "leaf"),
        P(("leaf", "rhs"), None, None),
        P(("leaf", "rhs"), None, None),
        P(("leaf", "rhs"), None, None, None),
        P(("leaf", "rhs"), None, None, None),
        P(),
        P(),
    )
    out_specs = P("rhs", "leaf")
    return jax.shard_map(shards, mesh=mesh, in_specs=in_specs, out_specs=out_specs, check_vma=False)
```

```python
import jax
import jax.numpy as jnp
from jax import lax
from jax.experimental import pallas as pl
from jax.experimental.pallas import tpu as pltpu
from jax.sharding import PartitionSpec as P

F32 = jnp.float32
BF16 = jnp.bfloat16
F16 = jnp.float16
VMEM = pl.BlockSpec(memory_space=pltpu.VMEM)
HBM = pl.BlockSpec(memory_space=pltpu.HBM)
LIMIT = 32 * 2**20
EXTRA = 16


def swap(value, axis, mask):
    pairs = [(source, source ^ mask) for source in range(lax.axis_size(axis))]
    return lax.ppermute(value, axis, pairs)


def split(value):
    high = value.astype(BF16)
    return high, (value - high.astype(F32)).astype(BF16)


def dot(a, b):
    return jnp.dot(a, b, preferred_element_type=F32)


def dot_narrow(value, matrix):
    rows = value.shape[0]
    both = dot(jnp.concatenate(split(value), axis=0), matrix)
    return both[:rows] + both[rows:]


def dot_wide(value, high_matrix, low_matrix):
    return dot_narrow(value, high_matrix) + dot(value.astype(BF16), low_matrix)


def encode(value):
    largest = jnp.max(jnp.abs(value), axis=0, keepdims=True)
    power = jnp.ceil(jnp.log2(jnp.maximum(largest, 1e-30))) - 14.0
    scaled = value * jnp.exp2(-power)
    return scaled, jnp.broadcast_to(power, (EXTRA, value.shape[1]))


def put_encoded(ref, value):
    rows = value.shape[0]
    ref[:rows, :], ref[rows:, :] = encode(value)


def decode(ref):
    rows = ref.shape[0] - EXTRA
    return ref[:rows, :] * jnp.exp2(ref[rows : rows + 1, :])


def call(body, outs, operands, flops=0, moved=0, **more):
    return pl.pallas_call(
        body,
        out_shape=outs,
        compiler_params=pltpu.CompilerParams(vmem_limit_bytes=LIMIT),
        cost_estimate=pl.CostEstimate(flops=flops, bytes_accessed=moved, transcendentals=0),
        **more,
    )(*operands)


def shape(*dims, dtype=F32):
    return jax.ShapeDtypeStruct(dims, dtype)


def line(message, axis, step, beside=None):
    leaves, group = lax.axis_size("leaf"), lax.axis_size("rhs")
    if axis == "leaf":
        pairs = [(i, i ^ step * (1 + (i & 1))) for i in range(leaves)]
    else:
        axis = ("leaf", "rhs")
        pairs = [(i * group + j, i * group + (j ^ (1 + (i & 1)))) for i in range(leaves) for j in range(group)]
    mine = lax.ppermute(message, axis, pairs)
    third = swap(message, "leaf" if axis == "leaf" else "rhs", 3 * step)
    if beside is not None:
        mine, beside = lax.optimization_barrier((mine, beside))
    return [mine, swap(mine, "leaf", 1), third], beside


def aligned(index, size):
    return pl.ds(pl.multiple_of(index * size, size), size)


def cut(vectors, leaf, masks):
    part = vectors.shape[0]

    def body(source, *rest):
        blocks, sems = rest[:-1], rest[-1]
        position = lax.axis_index("rhs")
        half = part // 2
        copies = [
            pltpu.make_async_copy(
                source.at[rows, aligned(position ^ mask, leaf)], block.at[rows, :], sems.at[2 * slot + side]
            )
            for slot, (mask, block) in enumerate(zip(masks, blocks))
            for side, rows in enumerate((slice(0, half), slice(half, part)))
        ]
        for copy in copies:
            copy.start()
        for copy in copies:
            copy.wait()

    count = len(masks)
    return call(
        body,
        [shape(part, leaf, dtype=BF16)] * count,
        (vectors,),
        moved=4 * count * part * leaf,
        in_specs=[HBM],
        out_specs=[VMEM] * count,
        scratch_shapes=[pltpu.SemaphoreType.DMA((2 * count,))],
    )


def oriented(coupling, is_right):
    wide = coupling.astype(F32)
    return jnp.where(is_right == 1, wide, wide.T).astype(BF16)


def transposed(matrix):
    return matrix.astype(F32).T.astype(BF16)


def times(matrix, parts):
    return dot(matrix, parts[0]) + dot(matrix, parts[1])


PICKS = [(0, 0), (0, 1), (1, 0), (1, 1), (1, 2), (1, 3), (2, 0), (2, 1), (3, 0), (3, 2), (3, 3)]
COUPLED = 5


def compose(vectors, leaf_basis, lower_transfer, lower_coupling, upper_transfer, upper_coupling):
    leaf, rank = leaf_basis.shape[1:]
    n_up = len(PICKS)
    n_all = n_up + COUPLED

    def body(vectors_hbm, basis_hbm, low_t_hbm, low_b_hbm, up_t_hbm, up_b_hbm, *rest):
        own_block, basis, lower_t, lower_down, coupled, pair, up_high, up_low, acc_high, acc_low, top_high, top_low = rest[:12]
        lower_b, uppers, couplings, sems = rest[12:]
        rhs_pos = lax.axis_index("rhs")
        node = lax.axis_index("leaf") + lax.axis_size("leaf")
        copies = {}

        def start(name, source, target):
            copies[name] = pltpu.make_async_copy(source, target, sems.at[len(copies)])
            copies[name].start()

        start("t", low_t_hbm.at[0], lower_t)
        start("b", low_b_hbm.at[0], lower_b)
        for slot, (height, mask) in enumerate(PICKS):
            start(slot, up_t_hbm.at[((node >> height) ^ mask) - 2], uppers.at[slot])
        for height in range(COUPLED):
            start(n_up + height, up_b_hbm.at[(node >> (height + 1)) - 1], couplings.at[height])
        start("basis", basis_hbm.at[0], basis)
        start("own", vectors_hbm.at[:, aligned(rhs_pos, leaf)], own_block)

        def upper(slot):
            copies[slot].wait()
            return uppers[slot]

        def coupling(height):
            copies[n_up + height].wait()
            return couplings[height]

        def put(high_ref, low_ref, slot, value):
            high, low = split(value)
            high_ref[aligned(slot, rank), :] = high
            low_ref[aligned(slot, rank), :] = low

        first = node & 1
        second = 1 - first

        copies["t"].wait()
        copies["b"].wait()
        for level in range(2):
            coupled[level] = oriented(lower_b[level], rhs_pos >> level & 1)
            lower_down[level] = transposed(lower_t[level])
        own2 = upper(0)
        pair[:rank, :] = own2
        pair[rank:, :] = upper(1)
        level3 = [upper(slot) for slot in range(2, 6)]
        own4, sib4, own5, third5, fourth5 = [upper(slot) for slot in range(6, 11)]
        coupled[2] = oriented(coupling(0), node & 1)
        down = transposed(own2)
        put(acc_high, acc_low, first, dot(oriented(coupling(1), node >> 1 & 1), down))
        down = split(dot(transposed(level3[0]), down))
        across = split(times(oriented(coupling(2), node >> 2 & 1), down))
        put(acc_high, acc_low, second, times(level3[2], across))
        put(acc_high, acc_low, 2, times(level3[3], across))
        down = split(times(transposed(own4), down))
        put(top_high, top_low, first, times(oriented(coupling(3), node >> 3 & 1), down))
        down = split(times(transposed(own5), down))
        across = split(times(oriented(coupling(4), node >> 4 & 1), down))
        put(top_high, top_low, second, times(third5, across))
        put(top_high, top_low, 2, times(fourth5, across))
        put(up_high, up_low, 0, dot(level3[0], own4))
        put(up_high, up_low, 1 + first, dot(level3[1], own4))
        put(up_high, up_low, 1 + second, dot(level3[2], sib4))
        put(up_high, up_low, 3, dot(level3[3], sib4))
        copies["basis"].wait()
        copies["own"].wait()

    stacked = [shape(n * rank, rank, dtype=BF16) for n in (2, 4, 4, 3, 3, 3, 3)]
    lower = shape(2, rank, rank, dtype=BF16)
    return call(
        body,
        [shape(vectors.shape[0], leaf, dtype=BF16), shape(leaf, rank, dtype=BF16), lower, lower, shape(3, rank, rank, dtype=BF16)] + stacked,
        (vectors, leaf_basis, lower_transfer, lower_coupling, upper_transfer, upper_coupling),
        flops=34 * 2 * rank**3,
        moved=2**22,
        in_specs=[HBM] * 6,
        out_specs=[VMEM] * 12,
        scratch_shapes=[
            pltpu.VMEM((2, rank, rank), BF16),
            pltpu.VMEM((n_up, rank, rank), BF16),
            pltpu.VMEM((COUPLED, rank, rank), BF16),
            pltpu.SemaphoreType.DMA((n_all + 4,)),
        ],
    )


def shards(
    vectors, near_blocks, leaf_basis, lower_transfer, lower_coupling, upper_transfer, upper_coupling
):
    part = vectors.shape[0]
    leaf, rank = leaf_basis.shape[1:]
    total = part * lax.axis_size("rhs")
    masks = (0, 1, 3, 2)

    vectors = pltpu.with_memory_space_constraint(vectors, pltpu.HBM)
    blocks = cut(vectors, leaf, masks[1:])
    came = [swap(block, "rhs", mask) for block, mask in zip(blocks, masks[1:])]
    leaf_basis, lower_transfer, lower_coupling, upper_transfer, upper_coupling = [
        pltpu.with_memory_space_constraint(array, pltpu.HBM)
        for array in (leaf_basis, lower_transfer, lower_coupling, upper_transfer, upper_coupling)
    ]
    own_block, basis, low, low_down, coupled, pair, up_high, up_low, acc_high, acc_low, top_high, top_low = compose(
        vectors, leaf_basis, lower_transfer, lower_coupling, upper_transfer, upper_coupling
    )
    message = shape(total + EXTRA, rank)

    def place(ref, value):
        position = lax.axis_index("rhs")
        for slot, mask in enumerate(masks):
            ref[aligned(position ^ mask, part), :] = value[slot * part : (slot + 1) * part, :]

    def leaf_body(own, first, second, third, basis_ref, transfer, cols, up_msg, coeff_ref, mid_ref, up_ref):
        for slot, ref in enumerate((own, first, second, third)):
            cols[slot * part : (slot + 1) * part, :] = ref[...]
        coeffs = dot(cols[...], basis_ref[...])
        place(coeff_ref, coeffs)
        middle = dot_narrow(coeffs, transfer[0])
        place(mid_ref, middle)
        upward = dot_narrow(middle, transfer[1])
        place(up_ref, upward)
        scaled, power = encode(upward)
        place(up_msg, scaled)
        up_msg[total:, :] = power

    plain = shape(total, rank)
    cols, up_msg, coeffs, middle, upward = call(
        leaf_body,
        (shape(total, leaf, dtype=BF16), message, plain, plain, plain),
        (own_block, *came, basis, low),
        flops=2 * total * leaf * rank,
        moved=2**21,
        in_specs=[VMEM] * 6,
        out_specs=[VMEM] * 5,
    )
    up_msg = up_msg.astype(F16)
    ups = [swap(up_msg, "rhs", mask).astype(F32) for mask in masks[1:]]

    def low_body(coeff_ref, mid_ref, low_msg):
        put_encoded(low_msg.at[: total + EXTRA, :], coeff_ref[...])
        put_encoded(low_msg.at[total + EXTRA :, :], mid_ref[...])

    low_msg = call(
        low_body,
        shape(2 * (total + EXTRA), rank),
        (coeffs, middle),
        moved=2**20,
        in_specs=[VMEM] * 2,
        out_specs=VMEM,
    )
    low_sib = swap(low_msg.astype(F16), "rhs", 1).astype(F32)

    def near_half(cols, half):
        width = leaf // 8

        def body(cols_ref, block_ref, out_ref):
            for step in range(4):
                rows = block_ref[0, (4 * half + step) * width : (4 * half + step + 1) * width, :]
                out_ref[:, step * width : (step + 1) * width] = lax.dot_general(
                    cols_ref[...], rows, (((1,), (1,)), ((), ())), preferred_element_type=F32
                )

        return call(
            body,
            shape(total, leaf // 2),
            (cols, near_blocks),
            flops=total * leaf * leaf,
            moved=leaf * leaf + 3 * total * leaf,
            in_specs=[VMEM] * 2,
            out_specs=VMEM,
        )

    def flip_body(basis_ref, out):
        for step in range(8):
            rows = slice(step * leaf // 8, (step + 1) * leaf // 8)
            out[:, rows] = basis_ref[rows, :].astype(F32).T.astype(BF16)

    flipped = call(
        flip_body,
        shape(rank, leaf, dtype=BF16),
        (basis,),
        moved=2**21,
        in_specs=[VMEM],
        out_specs=VMEM,
    )
    near_left = near_half(cols, 0)
    ups, near_left, flipped = lax.optimization_barrier((ups, near_left, flipped))

    def group_body(own, a, b, c, out):
        out[...] = own[...] + decode(a) + (decode(b) + decode(c))

    group = call(
        group_body,
        plain,
        (upward, *ups),
        moved=2**20,
        in_specs=[VMEM] * 4,
        out_specs=VMEM,
    )
    group_sib = swap(group, "leaf", 1)

    def chip_body(own, sibling, matrices, mid_ref, low_ref, out, kept, cousin_msg):
        value = dot_narrow(own[...], matrices[:rank, :]) + dot_narrow(sibling[...], matrices[rank:, :])
        kept[...] = value
        put_encoded(out, value)
        put_encoded(cousin_msg, mid_ref[...] + decode(low_ref.at[total + EXTRA :, :]))

    chip_msg, chip, cousin_msg = call(
        chip_body,
        (message, plain, message),
        (group, group_sib, pair, middle, low_sib),
        flops=8 * total * rank * rank,
        moved=2**20,
        in_specs=[VMEM] * 5,
        out_specs=[VMEM] * 3,
    )
    chip_msg = chip_msg.astype(F16)
    chips, _ = line(chip_msg, "leaf", 2)
    chips = [got.astype(F32) for got in chips]

    cousin_msg = cousin_msg.astype(F16)
    cousin = swap(cousin_msg, "rhs", 3).astype(F32)

    def line_body(own, a, b, c, high, low, out):
        value = jnp.concatenate([own[...]] + [decode(ref) for ref in (a, b, c)], axis=1)
        put_encoded(out, dot_wide(value, high[...], low[...]))

    line_msg = call(
        line_body,
        message,
        (chip, *chips, up_high, up_low),
        flops=24 * total * rank * rank,
        moved=2**21,
        in_specs=[VMEM] * 6,
        out_specs=VMEM,
    )
    line_msg, cols = lax.optimization_barrier((line_msg.astype(F16), cols))
    def partial_body(sibling, others, core, z1, z2, z3, pairs, high, low, at_leaf, at_pair, at_group):
        at_leaf[...] = dot_narrow(decode(sibling.at[: total + EXTRA, :]), pairs[0])
        at_pair[...] = dot_narrow(decode(others), pairs[1])
        value = jnp.concatenate([decode(ref) for ref in (z1, z2, z3)], axis=1)
        at_group[...] = dot_narrow(core[...], pairs[2]) + dot_wide(value, high[...], low[...])

    partials = call(
        partial_body,
        (plain, plain, plain),
        (low_sib, cousin, group_sib, *chips, coupled, acc_high, acc_low),
        flops=36 * total * rank * rank,
        moved=2**21,
        in_specs=[VMEM] * 9,
        out_specs=[VMEM] * 3,
    )
    lines, _ = line(line_msg, "leaf", 8)
    lines = [got.astype(F32) for got in lines]
    near_right = near_half(cols, 1)

    out_masks = (0, 2, 1, 3)

    def last_body(at_leaf, at_pair, at_group, a, b, c, high, low, steps, basis_ref, left, right, own, first, second, third, inner):
        position = lax.axis_index("rhs")
        value = jnp.concatenate([decode(ref) for ref in (a, b, c)], axis=1)
        value = at_group[...] + dot_wide(value, high[...], low[...])
        value = at_pair[...] + dot_narrow(value, steps[1])
        inner[...] = at_leaf[...] + dot_narrow(value, steps[0])
        coeffs = jnp.concatenate([inner[aligned(position ^ mask, part), :] for mask in masks], axis=0)
        far = dot(coeffs.astype(BF16), basis_ref[...])
        for mask, ref in zip(out_masks, (own, first, second, third)):
            slot = masks.index(mask)
            rows = slice(slot * part, (slot + 1) * part)
            ref[:, : leaf // 2] = (left[rows, :] + far[rows, : leaf // 2]).astype(ref.dtype)
            ref[:, leaf // 2 :] = (right[rows, :] + far[rows, leaf // 2 :]).astype(ref.dtype)

    sent = shape(part, leaf, dtype=BF16)
    own, *blocks = call(
        last_body,
        (shape(part, leaf), sent, sent, sent),
        (*partials, *lines, top_high, top_low, low_down, flipped, near_left, near_right),
        flops=2 * total * leaf * rank,
        moved=2**22,
        in_specs=[VMEM] * 12,
        out_specs=[VMEM] * 4,
        scratch_shapes=[pltpu.VMEM((total, rank), F32)],
    )
    blocks = [swap(block, "rhs", mask) for block, mask in zip(blocks, out_masks[1:])]

    def join_body(count, slots, *refs):
        blocks, out, wide, sems = refs[:count], refs[-3], refs[-2], refs[-1]
        position = lax.axis_index("rhs")
        copies = []
        for i, (block, slot) in enumerate(zip(blocks, slots)):
            wide[i] = block[...].astype(F32)
            target = out.at[:, aligned(position ^ out_masks[slot], leaf)]
            copies.append(pltpu.make_async_copy(wide.at[i], target, sems.at[i]))
            copies[-1].start()
        for copy in copies:
            copy.wait()

    def join(blocks, slots, under=None):
        count = len(blocks)

        def body(*refs):
            join_body(count, slots, *refs)

        return call(
            body,
            shape(part, 4 * leaf),
            (*blocks,) if under is None else (*blocks, under),
            moved=6 * part * leaf * count,
            in_specs=[VMEM] * count + ([] if under is None else [HBM]),
            out_specs=HBM,
            scratch_shapes=[pltpu.VMEM((count, part, leaf), F32), pltpu.SemaphoreType.DMA((count,))],
            input_output_aliases={} if under is None else {count: 0},
        )

    most = join((own, blocks[0], blocks[1]), (0, 1, 2))
    return join((blocks[2],), (3,), most)


def solution(mesh):
    in_specs = (
        P("rhs", "leaf"),
        P(("leaf", "rhs"), None, None),
        P(("leaf", "rhs"), None, None),
        P(("leaf", "rhs"), None, None, None),
        P(("leaf", "rhs"), None, None, None),
        P(),
        P(),
    )
    out_specs = P("rhs", "leaf")
    return jax.shard_map(shards, mesh=mesh, in_specs=in_specs, out_specs=out_specs, check_vma=False)
```
